32 devices in a mesh: tile: 16 (over z, y, core), seg: 2 (over x).
Axes of the slice: x: 2, y: 2, z: 4, core: 2. Of those that a mesh axis runs over, the one named last changes fastest.
Arguments:
- right_sides: float32 [65536, 512], P(('tile', 'seg')), may hold values from -6 to 6
- leaf_proj: float32 [16, 32, 64, 128], P('tile', 'seg'), may hold values from -0.5 to 0.5
- col_levels: float32 [16, 4, 16, 128, 128], P('tile', None, 'seg'), may hold values from -0.5 to 0.5
- middle_factor: float32 [16, 32, 64, 64], P('tile', 'seg'), may hold values from -0.75 to 0.75
- row_levels: float32 [16, 4, 16, 128, 128], P('tile', None, 'seg'), may hold values from -0.5 to 0.5
- leaf_expand: float32 [16, 32, 128, 64], P('tile', 'seg'), may hold values from -0.1875 to 0.1875
Outputs:
- product: float32 [4096, 512], P(('seg', 'tile'))
The draws below stay inside these ranges and needn't reach their ends.
All inputs are finite; a program needn't handle non-finite values.
Results may differ from the reference program's by a relative error of at most 0.0001.
Values sent between devices are 32-bit elements; how exact they have to be, the bound alone decides.
No kernel may reach another device: no remote copies, remote signals or barrier semaphores. Data moves between devices by JAX's collectives and lax.ppermute only.
A program may use at most 64 MiB of HBM per device.

```python
import jax
import jax.numpy as jnp
from jax import lax

K = 64
LEAF = 128
LVL = 4
R = 512
BOX = 16
TILES = 16
LEAVES = 32
PAIRS = 16
C = 4096
COLS = 65536
N_TILE = 16
N_SEG = 2


def block_levels(key, dims, cuts, low, top_value):
    loudness = 1.0
    for dim, shards_of in cuts:
        draws = jax.random.uniform(jax.random.fold_in(jax.random.fold_in(key, 6), dim), (shards_of,), jnp.float32, low / len(cuts), top_value / len(cuts))
        loudness = loudness * jnp.repeat(jnp.exp(draws), dims[dim] // shards_of).reshape((-1,) + (1,) * (len(dims) - 1 - dim))
    return loudness


def bell_draw(own_key, dims, scale, reach, cuts=(), dtype=jnp.bfloat16):
    array = jax.random.normal(own_key, dims, jnp.float32) * scale
    if len(cuts) > 0:
        array = block_levels(own_key, dims, cuts, -0.22, 0.18) * array
    return jnp.clip(array, min=-reach, max=reach).astype(dtype)


def setup_inputs(seed: int = 0) -> dict:
    seeds = jax.random.split(jax.random.key(seed), 7)
    return {
        "right_sides": bell_draw(seeds[0], (COLS, R), 1.0, 6.0, ((0, 32),), jnp.float32),
        "leaf_proj": bell_draw(seeds[1], (TILES, LEAVES, K, LEAF), LEAF ** -0.5, 0.5, ((0, 16), (1, 2)), jnp.float32),
        "col_levels": bell_draw(seeds[2], (TILES, LVL, PAIRS, 2 * K, 2 * K), (2 * K) ** -0.5, 0.5, ((0, 16), (2, 2)), jnp.float32),
        "middle_factor": bell_draw(seeds[3], (TILES, LEAVES, K, K), K ** -0.5, 0.75, ((0, 16), (1, 2)), jnp.float32),
        "row_levels": bell_draw(seeds[4], (TILES, LVL, PAIRS, 2 * K, 2 * K), (2 * K) ** -0.5, 0.5, ((0, 16), (2, 2)), jnp.float32),
        "leaf_expand": bell_draw(seeds[5], (TILES, LEAVES, LEAF, K), (K * N_TILE) ** -0.5, 0.1875, ((0, 16), (1, 2)), jnp.float32),
    }


def levels(coeffs, weights, groups):
    for level in range(LVL):
        stride = 2 ** level
        blocks = BOX // (2 * stride)
        wide = weights[level].reshape(groups, blocks, stride, 2, K, 2, K)
        split = coeffs.reshape(groups, blocks, 2, stride, K, R)
        mixed = jnp.einsum('gaeuvwx,gawexr->gauevr', wide, split, precision=lax.Precision.HIGHEST)
        coeffs = mixed.reshape(groups, BOX, K, R)
    return coeffs


def one_tile(columns, proj, col_weights, middle, row_weights, expand):
    coeffs = jnp.einsum('nkl,nlr->nkr', proj, columns.reshape(LEAVES, LEAF, R), precision=lax.Precision.HIGHEST)
    coeffs = levels(coeffs.reshape(N_SEG, BOX, K, R), col_weights, N_SEG)
    coeffs = jnp.einsum('nkj,njr->nkr', middle, coeffs.reshape(LEAVES, K, R), precision=lax.Precision.HIGHEST)
    coeffs = coeffs.reshape(N_SEG, N_SEG, BOX // N_SEG, K, R).transpose(1, 0, 2, 3, 4).reshape(N_SEG, BOX, K, R)
    coeffs = levels(coeffs, row_weights, N_SEG)
    rows = jnp.einsum('nlk,nkr->nlr', expand, coeffs.reshape(LEAVES, K, R), precision=lax.Precision.HIGHEST)
    return rows.reshape(C, R)


def reference(right_sides, leaf_proj, col_levels, middle_factor, row_levels, leaf_expand):
    def add_tile(total, pieces):
        return total + one_tile(*pieces), None

    stacked = (right_sides.reshape(TILES, C, R), leaf_proj, col_levels, middle_factor, row_levels, leaf_expand)
    total, _ = lax.scan(add_tile, jnp.zeros((C, R), jnp.float32), stacked)
    return total
```

```python
import functools

import jax
import jax.numpy as jnp
from jax import lax
from jax.experimental import pallas as pl
from jax.experimental.pallas import tpu as pltpu
from jax.sharding import PartitionSpec as P

F32 = jnp.float32
BF16 = jnp.bfloat16
CHUNK = 128


def split(x):
    hi = x.astype(BF16)
    return hi, (x - hi.astype(F32)).astype(BF16)


def dot(a, b, dims=((1,), (0,))):
    return lax.dot_general(a, b, (dims, ((), ())), preferred_element_type=F32)


def product3(w, v_hi, v_lo):
    w_hi, w_lo = split(w)
    wide = jnp.concatenate([w_hi, w_lo], axis=1)
    tall = jnp.concatenate([v_hi, v_hi], axis=0)
    return dot(wide, tall) + dot(w_hi, v_lo)


def rows_of(ref, start, size):
    return ref[pl.ds(start, size), :]


def pair_step(w, hi, lo, first, second, rank):
    v_hi = jnp.concatenate([rows_of(hi, first, rank), rows_of(hi, second, rank)], axis=0)
    v_lo = jnp.concatenate([rows_of(lo, first, rank), rows_of(lo, second, rank)], axis=0)
    out_hi, out_lo = split(product3(w, v_hi, v_lo))
    for place, half in ((first, 0), (second, 1)):
        hi[pl.ds(place, rank), :] = out_hi[half * rank:(half + 1) * rank]
        lo[pl.ds(place, rank), :] = out_lo[half * rank:(half + 1) * rank]


def column_kernel(n_seg, x_ref, proj_ref, col_ref, mid_ref, *refs):
    outs, (hi, lo) = refs[:n_seg], refs[n_seg:]
    box, rank, leaf = proj_ref.shape
    seg = lax.axis_index("seg")
    for n in range(box):
        x_hi, x_lo = split(x_ref[n * leaf:(n + 1) * leaf, :])
        c_hi, c_lo = split(product3(proj_ref[n], x_hi, x_lo))
        hi[n * rank:(n + 1) * rank, :] = c_hi
        lo[n * rank:(n + 1) * rank, :] = c_lo
    for level in range(col_ref.shape[0]):
        d = 2**level
        for j in range(box // 2):
            first = (j // d) * 2 * d + j % d
            pair_step(col_ref[level, j], hi, lo, first * rank, (first + d) * rank, rank)
    share = box // n_seg
    for delta in reversed(range(n_seg)):
        base = (seg ^ delta) * share
        for p in range(share):
            m_hi, m_lo = split(mid_ref[base + p])
            start = pl.multiple_of((base + p) * rank, rank)
            v_hi, v_lo = rows_of(hi, start, rank), rows_of(lo, start, rank)
            both = dot(jnp.concatenate([m_hi, m_lo], axis=0), v_hi)
            outs[delta][p * rank:(p + 1) * rank, :] = both[:rank] + both[rank:] + dot(m_hi, v_lo)


def row_kernel(n_seg, n_tile, *refs):
    ins, (row_ref, exp_ref, send_ref, keep_ref, hi, lo) = refs[:n_seg], refs[n_seg:]
    box, rank, leaf = exp_ref.shape
    share = box // n_seg
    seg = lax.axis_index("seg")
    tile = lax.axis_index("tile")
    levels = row_ref.shape[0]
    for delta in range(n_seg):
        base = (seg ^ delta) * share
        start = pl.multiple_of(base * rank, share * rank)
        v_hi, v_lo = split(ins[delta][...])
        hi[pl.ds(start, share * rank), :] = v_hi
        lo[pl.ds(start, share * rank), :] = v_lo
    for level in range(levels):
        d = 2**level
        for j in range(box // 2):
            first = (j // d) * 2 * d + j % d
            pair_step(row_ref[level, j], hi, lo, first * rank, (first + d) * rank, rank)
    out_rows = box * leaf // n_tile
    unit = min(out_rows, leaf)
    bits = n_tile.bit_length() - 1
    half = n_tile // 2
    for slot in reversed(range(n_tile)):
        relative = int(format(slot, f"0{bits}b")[::-1], 2)
        block = tile ^ relative
        for piece in range(out_rows // unit):
            n = (block * out_rows + piece * unit) // leaf
            start = pl.multiple_of(n * rank, rank)
            v_hi, v_lo = rows_of(hi, start, rank), rows_of(lo, start, rank)
            e_hi, e_lo = split(exp_ref[n])
            wide = jnp.concatenate([e_hi, e_lo, e_hi], axis=0)
            tall = jnp.concatenate([v_hi, v_hi, v_lo], axis=0)
            out = dot(wide, tall, ((0,), (0,)))
            if unit < leaf:
                parts = leaf // unit
                which = block % parts
                rows = out[:unit]
                for k in range(1, parts):
                    rows = jnp.where(which == k, out[k * unit:(k + 1) * unit], rows)
                out = rows
            target = send_ref if slot >= half else keep_ref
            at = (slot % half) * out_rows + piece * unit
            target[at:at + unit, :] = out


def shards(n_tile, n_seg, right_sides, leaf_proj, col_levels, middle_factor, row_levels, leaf_expand):
    proj, col, mid, row = leaf_proj[0], col_levels[0], middle_factor[0], row_levels[0]
    expand = jnp.swapaxes(leaf_expand[0], 1, 2)
    box, rank, leaf = proj.shape
    width = right_sides.shape[1]
    chunks = width // CHUNK
    out_rows = box * leaf // n_tile
    bits = n_tile.bit_length() - 1
    part = jax.ShapeDtypeStruct((box * rank // n_seg, CHUNK), F32)
    half = jax.ShapeDtypeStruct((box * leaf // 2, CHUNK), F32)
    scratch = [pltpu.VMEM((box * rank, CHUNK), BF16)] * 2
    params = pltpu.CompilerParams(vmem_limit_bytes=24 * 2**20)

    def whole(a):
        return pl.BlockSpec(a.shape, lambda i, r=len(a.shape): (0,) * r)

    def column_side(c):
        return pl.pallas_call(
            functools.partial(column_kernel, n_seg),
            grid=(1,),
            in_specs=[pl.BlockSpec((box * leaf, CHUNK), lambda i: (0, c)), whole(proj), whole(col), whole(mid)],
            out_specs=[whole(part)] * n_seg,
            out_shape=[part] * n_seg,
            scratch_shapes=scratch,
            compiler_params=params,
            cost_estimate=pl.CostEstimate(flops=600_000_000, bytes_accessed=5_000_000, transcendentals=0),
            name="column_side",
        )(right_sides, proj, col, mid)

    def row_side(parts):
        return pl.pallas_call(
            functools.partial(row_kernel, n_seg, n_tile),
            grid=(1,),
            in_specs=[whole(part)] * n_seg + [whole(row), whole(expand)],
            out_specs=[whole(half)] * 2,
            out_shape=[half] * 2,
            scratch_shapes=scratch,
            compiler_params=params,
            cost_estimate=pl.CostEstimate(flops=600_000_000, bytes_accessed=5_000_000, transcendentals=0),
            name="row_side",
        )(*parts, row, expand)

    def swap(x, axis, size, mask):
        return lax.ppermute(x, axis, [(i, i ^ mask) for i in range(size)])

    columns = []
    for c in range(chunks):
        parts = column_side(c)
        columns.append([parts[0]] + [swap(parts[k], "seg", n_seg, k) for k in range(1, n_seg)])
    results = []
    for c in range(chunks):
        send, keep = row_side(columns[c])
        terms = [keep]
        for b in range(bits):
            terms.append(swap(send, "tile", n_tile, 1 << b))
            low = (n_tile >> (b + 2)) * out_rows
            high = 2 * low if b + 1 < bits else out_rows
            send = sum(x[low:high] for x in terms[1:]) + terms[0][low:high]
        results.append(send)
    return jnp.concatenate(results, axis=1)


def solution(mesh):
    in_specs = (
        P(("tile", "seg"), None),
        P("tile", "seg", None, None),
        P("tile", None, "seg", None, None),
        P("tile", "seg", None, None),
        P("tile", None, "seg", None, None),
        P("tile", "seg", None, None),
    )
    out_specs = P(("seg", "tile"), None)
    body = functools.partial(shards, mesh.shape["tile"], mesh.shape["seg"])
    return jax.shard_map(body, mesh=mesh, in_specs=in_specs, out_specs=out_specs, check_vma=False)
```

```python
import functools

import jax
import jax.numpy as jnp
from jax import lax
from jax.experimental import pallas as pl
from jax.experimental.pallas import tpu as pltpu
from jax.sharding import PartitionSpec as P

F32 = jnp.float32
BF16 = jnp.bfloat16
CHUNK = 128


def split(x):
    hi = x.astype(BF16)
    return hi, (x - hi.astype(F32)).astype(BF16)


def dot(a, b, dims=((1,), (0,))):
    return lax.dot_general(a, b, (dims, ((), ())), preferred_element_type=F32)


def wide_of(w):
    return jnp.concatenate(split(w), axis=1)


def product3(wide, v_hi, v_lo):
    tall = jnp.concatenate([v_hi, v_hi], axis=0)
    return dot(wide, tall) + dot(wide[:, :v_hi.shape[0]], v_lo)


def rows_of(ref, start, size):
    return ref[pl.ds(start, size), :]


def level_step(level, wide_at, hi, lo, rank):
    d = 2**level
    for j in range(hi.shape[0] // (2 * rank)):
        first = ((j // d) * 2 * d + j % d) * rank
        second = first + d * rank
        v_hi = jnp.concatenate([rows_of(hi, first, rank), rows_of(hi, second, rank)], axis=0)
        v_lo = jnp.concatenate([rows_of(lo, first, rank), rows_of(lo, second, rank)], axis=0)
        out_hi, out_lo = split(product3(wide_at(j), v_hi, v_lo))
        for place, half in ((first, 0), (second, 1)):
            hi[pl.ds(place, rank), :] = out_hi[half * rank:(half + 1) * rank]
            lo[pl.ds(place, rank), :] = out_lo[half * rank:(half + 1) * rank]


def column_kernel(n_seg, start, x_hbm, proj_hbm, col_hbm, mid_hbm, *refs):
    outs, (x_ref, proj_ref, col_ref, mid_ref, hi, lo, sems) = refs[:-7], refs[-7:]
    box, rank, leaf = proj_ref.shape
    levels = col_ref.shape[0]
    width = x_ref.shape[1]
    pieces = 4
    per = box // pieces
    share = box // n_seg
    seg = lax.axis_index("seg")

    def x_copy(k):
        rows = pl.ds(k * per * leaf, per * leaf)
        return pltpu.make_async_copy(x_hbm.at[rows, pl.ds(start, width)], x_ref.at[rows, :], sems.at[k])

    proj_copy = pltpu.make_async_copy(proj_hbm, proj_ref, sems.at[pieces])
    col_copies = [pltpu.make_async_copy(col_hbm.at[k], col_ref.at[k], sems.at[pieces + 1 + k]) for k in range(levels)]
    mid_copy = pltpu.make_async_copy(mid_hbm, mid_ref, sems.at[pieces + 1 + levels])
    proj_copy.start()
    for k in range(pieces):
        x_copy(k).start()
    for copy in col_copies:
        copy.start()
    mid_copy.start()

    proj_copy.wait()
    for k in range(pieces):
        x_copy(k).wait()
        for n in range(k * per, (k + 1) * per):
            x_hi, x_lo = split(x_ref[n * leaf:(n + 1) * leaf, :])
            c_hi, c_lo = split(product3(wide_of(proj_ref[n]), x_hi, x_lo))
            hi[n * rank:(n + 1) * rank, :] = c_hi
            lo[n * rank:(n + 1) * rank, :] = c_lo
    for level in range(levels):
        col_copies[level].wait()
        level_step(level, lambda j: wide_of(col_ref[level, j]), hi, lo, rank)
    mid_copy.wait()
    for delta in reversed(range(n_seg)):
        base = (seg ^ delta) * share
        for p in range(share):
            m_hi, m_lo = split(mid_ref[base + p])
            at = pl.multiple_of((base + p) * rank, rank)
            v_hi, v_lo = rows_of(hi, at, rank), rows_of(lo, at, rank)
            both = dot(jnp.concatenate([m_hi, m_lo], axis=0), v_hi)
            out = both[:rank] + both[rank:] + dot(m_hi, v_lo)
            for k in range(width // CHUNK):
                outs[k * n_seg + delta][p * rank:(p + 1) * rank, :] = out[:, k * CHUNK:(k + 1) * CHUNK]


def weights_kernel(after_ref, row_ref, exp_ref, wide_ref, tall_ref):
    del after_ref
    for level in range(row_ref.shape[0]):
        for j in range(row_ref.shape[1]):
            wide_ref[level, j] = wide_of(row_ref[level, j])
    for n in range(exp_ref.shape[0]):
        e_hi, e_lo = split(exp_ref[n])
        tall_ref[n] = jnp.concatenate([e_hi, e_lo, e_hi], axis=0)


def row_kernel(n_seg, n_tile, leaf, *refs):
    ins, (row_ref, exp_ref, send_ref, keep_ref, hi, lo) = refs[:n_seg], refs[n_seg:]
    box = exp_ref.shape[0]
    rank = hi.shape[0] // box
    share = box // n_seg
    seg = lax.axis_index("seg")
    tile = lax.axis_index("tile")
    for delta in range(n_seg):
        base = (seg ^ delta) * share
        at = pl.multiple_of(base * rank, share * rank)
        v_hi, v_lo = split(ins[delta][...])
        hi[pl.ds(at, share * rank), :] = v_hi
        lo[pl.ds(at, share * rank), :] = v_lo
    for level in range(row_ref.shape[0]):
        level_step(level, lambda j: row_ref[level, j], hi, lo, rank)
    out_rows = box * leaf // n_tile
    unit = min(out_rows, leaf)
    bits = n_tile.bit_length() - 1
    half = n_tile // 2
    for slot in reversed(range(n_tile)):
        relative = int(format(slot, f"0{bits}b")[::-1], 2)
        block = tile ^ relative
        for piece in range(out_rows // unit):
            n = (block * out_rows + piece * unit) // leaf
            at = pl.multiple_of(n * rank, rank)
            v_hi, v_lo = rows_of(hi, at, rank), rows_of(lo, at, rank)
            out = dot(exp_ref[n], jnp.concatenate([v_hi, v_hi, v_lo], axis=0), ((0,), (0,)))
            if unit < leaf:
                which = block % (leaf // unit)
                rows = out[:unit]
                for k in range(1, leaf // unit):
                    rows = jnp.where(which == k, out[k * unit:(k + 1) * unit], rows)
                out = rows
            target = send_ref if slot >= half else keep_ref
            at = (slot % half) * out_rows + piece * unit
            target[at:at + unit, :] = out


def tie(x, *others):
    return lax.optimization_barrier((x, *others))[0]


def shards(n_tile, n_seg, right_sides, leaf_proj, col_levels, middle_factor, row_levels, leaf_expand):
    proj, col, mid, row = leaf_proj[0], col_levels[0], middle_factor[0], row_levels[0]
    expand = jnp.swapaxes(leaf_expand[0], 1, 2)
    box, rank, leaf = proj.shape
    levels, pairs = col.shape[:2]
    chunks = right_sides.shape[1] // CHUNK
    out_rows = box * leaf // n_tile
    bits = n_tile.bit_length() - 1
    part = jax.ShapeDtypeStruct((box * rank // n_seg, CHUNK), F32)
    half = jax.ShapeDtypeStruct((box * leaf // 2, CHUNK), F32)
    params = pltpu.CompilerParams(vmem_limit_bytes=16 * 2**20)
    greedy = pltpu.CompilerParams(vmem_limit_bytes=53 * 2**20)
    cost = pl.CostEstimate(flops=600_000_000, bytes_accessed=5_000_000, transcendentals=0)
    in_hbm = pl.BlockSpec(memory_space=pltpu.HBM)
    in_vmem = pl.BlockSpec(memory_space=pltpu.VMEM)
    anywhere = pl.BlockSpec(memory_space=pl.ANY)

    def column_side(start, count):
        width = count * CHUNK
        outs = pl.pallas_call(
            functools.partial(column_kernel, n_seg, start * CHUNK),
            in_specs=[in_hbm] * 4,
            out_specs=[in_vmem] * (n_seg * count),
            out_shape=[part] * (n_seg * count),
            scratch_shapes=[
                pltpu.VMEM((box * leaf, width), F32),
                pltpu.VMEM(proj.shape, F32),
                pltpu.VMEM(col.shape, F32),
                pltpu.VMEM(mid.shape, F32),
                pltpu.VMEM((box * rank, width), BF16),
                pltpu.VMEM((box * rank, width), BF16),
                pltpu.SemaphoreType.DMA((6 + levels,)),
            ],
            compiler_params=greedy,
            cost_estimate=cost,
            name="column_side",
        )(right_sides, proj, col, mid)
        return [outs[k * n_seg:(k + 1) * n_seg] for k in range(count)]

    def row_weights(after):
        return pl.pallas_call(
            weights_kernel,
            in_specs=[anywhere, in_vmem, in_vmem],
            out_specs=[in_vmem] * 2,
            out_shape=[
                jax.ShapeDtypeStruct((levels, pairs, 2 * rank, 4 * rank), BF16),
                jax.ShapeDtypeStruct((box, 3 * rank, leaf), BF16),
            ],
            compiler_params=params,
            cost_estimate=cost,
            name="row_weights",
        )(after, row, expand)

    def row_side(parts, weights):
        return pl.pallas_call(
            functools.partial(row_kernel, n_seg, n_tile, leaf),
            in_specs=[in_vmem] * (n_seg + 2),
            out_specs=[in_vmem] * 2,
            out_shape=[half] * 2,
            scratch_shapes=[pltpu.VMEM((box * rank, CHUNK), BF16)] * 2,
            compiler_params=params,
            cost_estimate=cost,
            name="row_side",
        )(*parts, *weights)

    def swap(x, axis, size, mask):
        return lax.ppermute(x, axis, [(i, i ^ mask) for i in range(size)])

    def exchange(parts, *after):
        return [parts[0]] + [swap(tie(parts[k], *after) if after else parts[k], "seg", n_seg, k) for k in range(1, n_seg)]

    def total(terms, low, high):
        return functools.reduce(jnp.add, [x[low:high] for x in terms])

    def next_send(terms):
        left = terms[-1].shape[0]
        return total(terms, left // 2, left)

    parts = column_side(0, 1)
    received = {0: exchange(parts[0])}
    if chunks > 1:
        parts += column_side(1, chunks - 1)
        received[1] = exchange(parts[1])
    weights = row_weights(parts[-1][0])

    terms, sends = [], {}
    for c in range(chunks):
        after = [sends[c - 2, 2]] if c >= 2 else []
        arrived = [tie(x, *after) if after else x for x in received[c]]
        send, keep = row_side(arrived, weights)
        terms.append([keep, swap(send, "tile", n_tile, 1)])
        sends[c, 1] = next_send(terms[c])
        terms[c].append(swap(sends[c, 1], "tile", n_tile, 2))
        if c + 2 < chunks:
            received[c + 2] = exchange(parts[c + 2], sends[c, 1])
        if c >= 1:
            sends[c - 1, 2] = tie(next_send(terms[c - 1]), sends[c, 1])
            terms[c - 1].append(swap(sends[c - 1, 2], "tile", n_tile, 4))
    last = chunks - 1
    sends[last, 2] = next_send(terms[last])
    terms[last].append(swap(sends[last, 2], "tile", n_tile, 4))
    for c in range(chunks):
        for b in range(3, bits):
            sends[c, b] = next_send(terms[c])
            if c < last:
                sends[c, b] = tie(sends[c, b], sends[last, 1])
            terms[c].append(swap(sends[c, b], "tile", n_tile, 1 << b))
    return jnp.concatenate([total(t, 0, out_rows) for t in terms], axis=1)


def solution(mesh):
    in_specs = (
        P(("tile", "seg"), None),
        P("tile", "seg", None, None),
        P("tile", None, "seg", None, None),
        P("tile", "seg", None, None),
        P("tile", None, "seg", None, None),
        P("tile", "seg", None, None),
    )
    out_specs = P(("seg", "tile"), None)
    body = functools.partial(shards, mesh.shape["tile"], mesh.shape["seg"])
    return jax.shard_map(body, mesh=mesh, in_specs=in_specs, out_specs=out_specs, check_vma=False)
```

```python
import functools

import jax
import jax.numpy as jnp
from jax import lax
from jax.experimental import pallas as pl
from jax.experimental.pallas import tpu as pltpu
from jax.sharding import PartitionSpec as P

F32 = jnp.float32
BF16 = jnp.bfloat16
CHUNK = 128


def split(x):
    hi = x.astype(BF16)
    return hi, (x - hi.astype(F32)).astype(BF16)


def dot(a, b, dims=((1,), (0,))):
    return lax.dot_general(a, b, (dims, ((), ())), preferred_element_type=F32)


def wide_of(w):
    return jnp.concatenate(split(w), axis=1)


def product3(wide, v_hi, v_lo):
    depth, width = v_hi.shape
    if width > CHUNK:
        return dot(wide, jnp.concatenate([v_hi, v_hi], axis=0)) + dot(wide[:, :depth], v_lo)
    left = jnp.concatenate([v_hi, v_hi], axis=0)
    right = jnp.concatenate([v_lo, jnp.zeros_like(v_lo)], axis=0)
    both = dot(wide, jnp.concatenate([left, right], axis=1))
    return both[:, :width] + both[:, width:]


def pair_of(hi, lo, first, second, rank, cols=slice(None)):
    return [jnp.concatenate([x[pl.ds(first, rank), cols], x[pl.ds(second, rank), cols]], axis=0) for x in (hi, lo)]


def level_step(level, wide_at, hi, lo, rank, cuts):
    d = 2**level
    for j in range(hi.shape[0] // (2 * rank)):
        first = ((j // d) * 2 * d + j % d) * rank
        second = first + d * rank
        wide = wide_at(j)
        for cols in cuts:
            out_hi, out_lo = split(product3(wide, *pair_of(hi, lo, first, second, rank, cols)))
            for place, half in ((first, 0), (second, 1)):
                hi[pl.ds(place, rank), cols] = out_hi[half * rank:(half + 1) * rank]
                lo[pl.ds(place, rank), cols] = out_lo[half * rank:(half + 1) * rank]


def cuts_of(width):
    odd = width % (2 * CHUNK)
    return ([slice(0, odd)] if odd else []) + [slice(k, k + 2 * CHUNK) for k in range(odd, width, 2 * CHUNK)]


def column_kernel(n_seg, start, x_hbm, proj_hbm, col_hbm, mid_hbm, *refs):
    outs, (x_ref, proj_ref, col_ref, mid_ref, hi, lo, sems) = refs[:-7], refs[-7:]
    box, rank, leaf = proj_ref.shape
    levels = col_ref.shape[0]
    width = x_ref.shape[1]
    cuts = cuts_of(width)
    pieces = 4
    per = box // pieces
    share = box // n_seg
    seg = lax.axis_index("seg")

    def x_copy(k):
        rows = pl.ds(k * per * leaf, per * leaf)
        return pltpu.make_async_copy(x_hbm.at[rows, pl.ds(start, width)], x_ref.at[rows, :], sems.at[k])

    proj_copy = pltpu.make_async_copy(proj_hbm, proj_ref, sems.at[pieces])
    col_copies = [pltpu.make_async_copy(col_hbm.at[k], col_ref.at[k], sems.at[pieces + 1 + k]) for k in range(levels)]
    mid_copy = pltpu.make_async_copy(mid_hbm, mid_ref, sems.at[pieces + 1 + levels])
    proj_copy.start()
    for k in range(pieces):
        x_copy(k).start()
    for copy in col_copies:
        copy.start()
    mid_copy.start()

    proj_copy.wait()
    for k in range(pieces):
        x_copy(k).wait()
        for n in range(k * per, (k + 1) * per):
            wide = wide_of(proj_ref[n])
            for cols in cuts:
                c_hi, c_lo = split(product3(wide, *split(x_ref[n * leaf:(n + 1) * leaf, cols])))
                hi[n * rank:(n + 1) * rank, cols] = c_hi
                lo[n * rank:(n + 1) * rank, cols] = c_lo
    for level in range(levels):
        col_copies[level].wait()
        level_step(level, lambda j: wide_of(col_ref[level, j]), hi, lo, rank, cuts)
    mid_copy.wait()
    for delta in reversed(range(n_seg)):
        base = (seg ^ delta) * share
        for p in range(share):
            wide = wide_of(mid_ref[base + p])
            at = pl.multiple_of((base + p) * rank, rank)
            for cols in cuts:
                out = product3(wide, hi[pl.ds(at, rank), cols], lo[pl.ds(at, rank), cols])
                for k in range(out.shape[1] // CHUNK):
                    target = outs[(cols.start // CHUNK + k) * n_seg + delta]
                    target[p * rank:(p + 1) * rank, :] = out[:, k * CHUNK:(k + 1) * CHUNK]


def slots_of(n_tile, box, leaf):
    bits = n_tile.bit_length() - 1
    out_rows = box * leaf // n_tile
    relative = [int(format(slot, f"0{bits}b")[::-1], 2) for slot in range(n_tile)]
    return relative, out_rows, min(out_rows, leaf), max(1, out_rows // leaf)


def weights_kernel(row_ref, wide_ref):
    for level in range(row_ref.shape[0]):
        for j in range(row_ref.shape[1]):
            wide_ref[level, j] = wide_of(row_ref[level, j])


def expand_weights_kernel(n_tile, exp_ref, other_ref, last_ref):
    box, _, leaf = exp_ref.shape
    tile = lax.axis_index("tile")
    relative, out_rows, unit, pieces = slots_of(n_tile, box, leaf)
    for slot in range(n_tile // 2):
        block = tile ^ relative[slot]
        for piece in range(pieces):
            n = (block * out_rows + piece * unit) // leaf
            both = jnp.concatenate([exp_ref[n], other_ref[n]], axis=0).T
            rows = both[:unit]
            for k in range(1, leaf // unit):
                rows = jnp.where(block % (leaf // unit) == k, both[k * unit:(k + 1) * unit], rows)
            last_ref[slot * pieces + piece] = wide_of(rows)


def row_kernel(n_seg, n_tile, leaf, *refs):
    ins, (row_ref, *outs, hi, lo, full) = refs[:n_seg], refs[n_seg:]
    levels, pairs = row_ref.shape[:2]
    box = 2 * pairs
    rank = hi.shape[0] // box
    share = box // n_seg
    seg = lax.axis_index("seg")
    tile = lax.axis_index("tile")
    for delta in range(n_seg):
        base = (seg ^ delta) * share
        at = pl.multiple_of(base * rank, share * rank)
        v_hi, v_lo = split(ins[delta][...])
        hi[pl.ds(at, share * rank), :] = v_hi
        lo[pl.ds(at, share * rank), :] = v_lo
    for level in range(levels - 1):
        level_step(level, lambda j: row_ref[level, j], hi, lo, rank, [slice(None)])
    for j in range(pairs):
        second = (j + pairs) * rank
        out = product3(row_ref[levels - 1, j], *pair_of(hi, lo, j * rank, second, rank))
        full[j * rank:(j + 1) * rank, :] = out[:rank]
        full[second:second + rank, :] = out[rank:]
    relative, out_rows, unit, pieces = slots_of(n_tile, box, leaf)
    group = n_tile // 4
    for slot in range(n_tile):
        block = tile ^ relative[slot]
        for piece in range(pieces):
            n = (block * out_rows + piece * unit) // leaf
            at = (slot % group * pieces + piece) * rank
            outs[slot // group][at:at + rank, :] = full[pl.ds(pl.multiple_of(n * rank, rank), rank), :]


def expand_kernel(part, own_ref, other_ref, last_ref, out_ref):
    rank = last_ref.shape[2] // 4
    unit = last_ref.shape[1]
    for k in range(own_ref.shape[0] // rank):
        rows = slice(k * rank, (k + 1) * rank)
        v = jnp.concatenate([own_ref[rows, :], other_ref[rows, :]], axis=0)
        wide = last_ref[part * own_ref.shape[0] // rank + k]
        out_ref[k * unit:(k + 1) * unit, :] = product3(wide, *split(v))


def tie(x, *others):
    return lax.optimization_barrier((x, *others))[0]


def shards(n_tile, n_seg, right_sides, leaf_proj, col_levels, middle_factor, row_levels, leaf_expand):
    proj, col, mid, row = leaf_proj[0], col_levels[0], middle_factor[0], row_levels[0]
    expand = jnp.swapaxes(leaf_expand[0], 1, 2)
    box, rank, leaf = proj.shape
    levels, pairs = col.shape[:2]
    chunks = right_sides.shape[1] // CHUNK
    _, out_rows, unit, pieces = slots_of(n_tile, box, leaf)
    bits = n_tile.bit_length() - 1
    part = jax.ShapeDtypeStruct((box * rank // n_seg, CHUNK), F32)
    quarter = jax.ShapeDtypeStruct((n_tile // 4 * pieces * rank, CHUNK), F32)
    summed = jax.ShapeDtypeStruct((box * leaf // 4, CHUNK), F32)
    params = pltpu.CompilerParams(vmem_limit_bytes=16 * 2**20)
    cost = pl.CostEstimate(flops=1_000_000, bytes_accessed=100_000, transcendentals=0)
    in_hbm = pl.BlockSpec(memory_space=pltpu.HBM)
    in_vmem = pl.BlockSpec(memory_space=pltpu.VMEM)

    def column_side(start, count, mid, limit=53):
        width = count * CHUNK
        outs = pl.pallas_call(
            functools.partial(column_kernel, n_seg, start * CHUNK),
            in_specs=[in_hbm] * 4,
            out_specs=[in_vmem] * (n_seg * count),
            out_shape=[part] * (n_seg * count),
            scratch_shapes=[
                pltpu.VMEM((box * leaf, width), F32),
                pltpu.VMEM(proj.shape, F32),
                pltpu.VMEM(col.shape, F32),
                pltpu.VMEM(mid.shape, F32),
                pltpu.VMEM((box * rank, width), BF16),
                pltpu.VMEM((box * rank, width), BF16),
                pltpu.SemaphoreType.DMA((6 + levels,)),
            ],
            compiler_params=pltpu.CompilerParams(vmem_limit_bytes=limit * 2**20),
            cost_estimate=cost,
            name="column_side",
        )(right_sides, proj, col, mid)
        return [outs[k * n_seg:(k + 1) * n_seg] for k in range(count)]

    def row_weights():
        return pl.pallas_call(
            weights_kernel,
            in_specs=[in_vmem],
            out_specs=in_vmem,
            out_shape=jax.ShapeDtypeStruct((levels, pairs, 2 * rank, 4 * rank), BF16),
            compiler_params=params,
            cost_estimate=cost,
            name="row_weights",
        )(row)

    def expand_weights(other):
        return pl.pallas_call(
            functools.partial(expand_weights_kernel, n_tile),
            in_specs=[in_vmem] * 2,
            out_specs=in_vmem,
            out_shape=jax.ShapeDtypeStruct((n_tile // 2 * pieces, unit, 4 * rank), BF16),
            compiler_params=params,
            cost_estimate=cost,
            name="expand_weights",
        )(expand, other)

    def row_side(parts, wide):
        return pl.pallas_call(
            functools.partial(row_kernel, n_seg, n_tile, leaf),
            in_specs=[in_vmem] * (n_seg + 1),
            out_specs=[in_vmem] * 4,
            out_shape=[quarter] * 4,
            scratch_shapes=[pltpu.VMEM((box * rank, CHUNK), t) for t in (BF16, BF16, F32)],
            compiler_params=params,
            cost_estimate=pl.CostEstimate(flops=20_000_000_000, bytes_accessed=100_000, transcendentals=0),
            name="row_side",
        )(*parts, wide)

    def expanded(part, own, other, last):
        return pl.pallas_call(
            functools.partial(expand_kernel, part),
            in_specs=[in_vmem] * 3,
            out_specs=in_vmem,
            out_shape=summed,
            compiler_params=params,
            cost_estimate=cost,
            name="expand",
        )(own, other, last)

    def swap(x, axis, size, mask):
        return lax.ppermute(x, axis, [(i, i ^ mask) for i in range(size)])

    def exchange(parts, *after):
        return [parts[0]] + [swap(tie(parts[k], *after) if after else parts[k], "seg", n_seg, k) for k in range(1, n_seg)]

    def total(terms, low, high):
        return functools.reduce(jnp.add, [x[low:high] for x in terms])

    def next_send(terms):
        left = terms[-1].shape[0]
        return total(terms, left // 2, left)

    parts = column_side(0, 1, mid)
    received = {0: exchange(parts[0])}
    if chunks > 1:
        parts += column_side(1, chunks - 1, tie(mid, parts[0][-1]), 52)
        received[1] = exchange(parts[1])
    wide = row_weights()
    last_wide = expand_weights(swap(tie(expand, parts[-1][0]), "tile", n_tile, 1))

    terms, sends, lows = [], {}, []
    last = chunks - 1
    for c in range(chunks):
        after = [sends[k] for k in ((c - 1, 1), (c - 2, 2)) if k in sends] or [parts[-1][0]]
        own_low, own_high, low, high = row_side([tie(x, *after) for x in received[c]], wide)
        lows.append((own_low, swap(low, "tile", n_tile, 1)))
        got = swap(high, "tile", n_tile, 1)
        if c:
            own, other = lows[c - 1]
            terms[c - 1][0] = expanded(0, own, tie(other, own_high), last_wide)
            got = tie(got, terms[c - 1][0])
            sends[c - 1, 2] = next_send(terms[c - 1])
            if c == last:
                got = tie(got, sends[c - 1, 2])
        sends[c, 1] = expanded(1, own_high, got, last_wide)
        terms.append([None, swap(sends[c, 1], "tile", n_tile, 2)])
        if c + 2 < chunks:
            received[c + 2] = exchange(parts[c + 2], sends[c, 1])
        if c:
            if c < last:
                sends[c - 1, 2] = tie(sends[c - 1, 2], sends[c, 1])
            terms[c - 1].append(swap(sends[c - 1, 2], "tile", n_tile, 4))
    own, other = lows[last]
    terms[last][0] = expanded(0, own, tie(other, sends[last, 1]), last_wide)
    sends[last, 2] = next_send(terms[last])
    terms[last].append(swap(sends[last, 2], "tile", n_tile, 4))
    for c in range(chunks):
        for b in range(3, bits):
            sends[c, b] = next_send(terms[c])
            if c < last:
                sends[c, b] = tie(sends[c, b], sends[last, 1])
            terms[c].append(swap(sends[c, b], "tile", n_tile, 1 << b))
    return jnp.concatenate([total(t, 0, out_rows) for t in terms], axis=1)


def solution(mesh):
    in_specs = (
        P(("tile", "seg"), None),
        P("tile", "seg", None, None),
        P("tile", None, "seg", None, None),
        P("tile", "seg", None, None),
        P("tile", None, "seg", None, None),
        P("tile", "seg", None, None),
    )
    out_specs = P(("seg", "tile"), None)
    body = functools.partial(shards, mesh.shape["tile"], mesh.shape["seg"])
    return jax.shard_map(body, mesh=mesh, in_specs=in_specs, out_specs=out_specs, check_vma=False)
```

```python
import functools

import jax
import jax.numpy as jnp
from jax import lax
from jax.experimental import pallas as pl
from jax.experimental.pallas import tpu as pltpu
from jax.sharding import PartitionSpec as P

F32 = jnp.float32
BF16 = jnp.bfloat16
CHUNK = 128


def split(x):
    hi = x.astype(BF16)
    return hi, (x - hi.astype(F32)).astype(BF16)


def dot(a, b, dims=((1,), (0,))):
    return lax.dot_general(a, b, (dims, ((), ())), preferred_element_type=F32)


def wide_of(w):
    return jnp.concatenate(split(w), axis=1)


def product3(wide, v_hi, v_lo):
    depth, width = v_hi.shape
    if width > CHUNK:
        return dot(wide, jnp.concatenate([v_hi, v_hi], axis=0)) + dot(wide[:, :depth], v_lo)
    left = jnp.concatenate([v_hi, v_hi], axis=0)
    right = jnp.concatenate([v_lo, jnp.zeros_like(v_lo)], axis=0)
    both = dot(wide, jnp.concatenate([left, right], axis=1))
    return both[:, :width] + both[:, width:]


def pair_of(hi, lo, first, second, rank, cols=slice(None)):
    return [jnp.concatenate([x[pl.ds(first, rank), cols], x[pl.ds(second, rank), cols]], axis=0) for x in (hi, lo)]


def level_step(level, wide_at, hi, lo, rank, cuts):
    d = 2**level
    for j in range(hi.shape[0] // (2 * rank)):
        first = ((j // d) * 2 * d + j % d) * rank
        second = first + d * rank
        wide = wide_at(j)
        for cols in cuts:
            out_hi, out_lo = split(product3(wide, *pair_of(hi, lo, first, second, rank, cols)))
            for place, half in ((first, 0), (second, 1)):
                hi[pl.ds(place, rank), cols] = out_hi[half * rank:(half + 1) * rank]
                lo[pl.ds(place, rank), cols] = out_lo[half * rank:(half + 1) * rank]


def cuts_of(width):
    odd = width % (2 * CHUNK)
    return ([slice(0, odd)] if odd else []) + [slice(k, k + 2 * CHUNK) for k in range(odd, width, 2 * CHUNK)]


def project(n, wide, x, hi, lo, cuts):
    rank, leaf = wide.shape[0], wide.shape[1] // 2
    for cols in cuts:
        c_hi, c_lo = split(product3(wide, *split(x[n * leaf:(n + 1) * leaf, cols])))
        hi[n * rank:(n + 1) * rank, cols] = c_hi
        lo[n * rank:(n + 1) * rank, cols] = c_lo


def middle(n_seg, mid, outs, hi, lo, cuts):
    box, rank = mid.shape[:2]
    share = box // n_seg
    seg = lax.axis_index("seg")
    for delta in reversed(range(n_seg)):
        base = (seg ^ delta) * share
        for p in range(share):
            wide = wide_of(mid[base + p])
            at = pl.multiple_of((base + p) * rank, rank)
            for cols in cuts:
                out = product3(wide, hi[pl.ds(at, rank), cols], lo[pl.ds(at, rank), cols])
                for k in range(out.shape[1] // CHUNK):
                    target = outs[(cols.start // CHUNK + k) * n_seg + delta]
                    target[p * rank:(p + 1) * rank, :] = out[:, k * CHUNK:(k + 1) * CHUNK]


def column_kernel(n_seg, pieces, start, x_hbm, proj_hbm, col_hbm, mid_hbm, *refs):
    outs, (x_ref, proj_ref, col_ref, mid_ref, hi, lo, sems) = refs[:-7], refs[-7:]
    box, rank, leaf = proj_ref.shape
    levels, pairs = col_ref.shape[:2]
    width = x_ref.shape[1]
    per = box // pieces
    copies = []

    def fetch(src, dst):
        copies.append(pltpu.make_async_copy(src, dst, sems.at[len(copies)]))
        copies[-1].start()
        return copies[-1]

    first = []
    for k in range(pieces):
        rows = pl.ds(k * per * leaf, per * leaf)
        leaves = pl.ds(k * per, per)
        first.append((
            fetch(proj_hbm.at[leaves], proj_ref.at[leaves]),
            fetch(x_hbm.at[rows, pl.ds(start, width)], x_ref.at[rows, :]),
        ))
    halves = [pl.ds(k * (pairs // 2), pairs // 2) for k in range(2)]
    cols = [[fetch(col_hbm.at[k, h], col_ref.at[k, h]) for h in halves] for k in range(levels)]
    mid = fetch(mid_hbm, mid_ref)

    cuts = cuts_of(width)
    for k in range(pieces):
        for copy in first[k]:
            copy.wait()
        for n in range(k * per, (k + 1) * per):
            project(n, wide_of(proj_ref[n]), x_ref, hi, lo, cuts)
    for level in range(levels):
        for copy in cols[level]:
            copy.wait()
        level_step(level, lambda j: wide_of(col_ref[level, j]), hi, lo, rank, cuts)
    mid.wait()
    middle(n_seg, mid_ref, outs, hi, lo, cuts)


def slots_of(n_tile, box, leaf):
    bits = n_tile.bit_length() - 1
    out_rows = box * leaf // n_tile
    relative = [int(format(slot, f"0{bits}b")[::-1], 2) for slot in range(n_tile)]
    return relative, out_rows, min(out_rows, leaf), max(1, out_rows // leaf)


def weights_kernel(row_ref, wide_ref):
    for level in range(row_ref.shape[0]):
        for j in range(row_ref.shape[1]):
            wide_ref[level, j] = wide_of(row_ref[level, j])


def expand_weights_kernel(n_tile, exp_ref, other_ref, last_ref):
    box, _, leaf = exp_ref.shape
    tile = lax.axis_index("tile")
    relative, out_rows, unit, pieces = slots_of(n_tile, box, leaf)
    for slot in range(n_tile // 2):
        block = tile ^ relative[slot]
        for piece in range(pieces):
            n = (block * out_rows + piece * unit) // leaf
            both = jnp.concatenate([exp_ref[n], other_ref[n]], axis=0).T
            rows = both[:unit]
            for k in range(1, leaf // unit):
                rows = jnp.where(block % (leaf // unit) == k, both[k * unit:(k + 1) * unit], rows)
            last_ref[slot * pieces + piece] = wide_of(rows)


def row_kernel(n_seg, n_tile, leaf, *refs):
    ins, (row_ref, *outs, hi, lo, full) = refs[:n_seg], refs[n_seg:]
    levels, pairs = row_ref.shape[:2]
    box = 2 * pairs
    rank = hi.shape[0] // box
    share = box // n_seg
    seg = lax.axis_index("seg")
    tile = lax.axis_index("tile")
    for delta in range(n_seg):
        base = (seg ^ delta) * share
        at = pl.multiple_of(base * rank, share * rank)
        v_hi, v_lo = split(ins[delta][...])
        hi[pl.ds(at, share * rank), :] = v_hi
        lo[pl.ds(at, share * rank), :] = v_lo
    for level in range(levels - 1):
        level_step(level, lambda j: row_ref[level, j], hi, lo, rank, [slice(None)])
    for j in range(pairs):
        second = (j + pairs) * rank
        out = product3(row_ref[levels - 1, j], *pair_of(hi, lo, j * rank, second, rank))
        full[j * rank:(j + 1) * rank, :] = out[:rank]
        full[second:second + rank, :] = out[rank:]
    relative, out_rows, unit, pieces = slots_of(n_tile, box, leaf)
    group = n_tile // 4
    for slot in range(n_tile):
        block = tile ^ relative[slot]
        for piece in range(pieces):
            n = (block * out_rows + piece * unit) // leaf
            at = (slot % group * pieces + piece) * rank
            outs[slot // group][at:at + rank, :] = full[pl.ds(pl.multiple_of(n * rank, rank), rank), :]


def expand_kernel(part, own_ref, other_ref, last_ref, out_ref):
    rank = last_ref.shape[2] // 4
    unit = last_ref.shape[1]
    for k in range(own_ref.shape[0] // rank):
        rows = slice(k * rank, (k + 1) * rank)
        v = jnp.concatenate([own_ref[rows, :], other_ref[rows, :]], axis=0)
        wide = last_ref[part * own_ref.shape[0] // rank + k]
        out_ref[k * unit:(k + 1) * unit, :] = product3(wide, *split(v))


def tie(x, *others):
    return lax.optimization_barrier((x, *others))[0]


def shards(n_tile, n_seg, right_sides, leaf_proj, col_levels, middle_factor, row_levels, leaf_expand):
    proj, col, mid, row = leaf_proj[0], col_levels[0], middle_factor[0], row_levels[0]
    expand = jnp.swapaxes(leaf_expand[0], 1, 2)
    box, rank, leaf = proj.shape
    levels, pairs = col.shape[:2]
    chunks = right_sides.shape[1] // CHUNK
    _, out_rows, unit, pieces = slots_of(n_tile, box, leaf)
    bits = n_tile.bit_length() - 1
    part = jax.ShapeDtypeStruct((box * rank // n_seg, CHUNK), F32)
    quarter = jax.ShapeDtypeStruct((n_tile // 4 * pieces * rank, CHUNK), F32)
    summed = jax.ShapeDtypeStruct((box * leaf // 4, CHUNK), F32)
    params = pltpu.CompilerParams(vmem_limit_bytes=16 * 2**20)
    cost = pl.CostEstimate(flops=1_000_000, bytes_accessed=100_000, transcendentals=0)
    in_hbm = pl.BlockSpec(memory_space=pltpu.HBM)
    in_vmem = pl.BlockSpec(memory_space=pltpu.VMEM)

    def column_side(start, count, mid, limit):
        pieces = 4
        width = count * CHUNK
        outs = pl.pallas_call(
            functools.partial(column_kernel, n_seg, pieces, start * CHUNK),
            in_specs=[in_hbm] * 4,
            out_specs=[in_vmem] * (n_seg * count),
            out_shape=[part] * (n_seg * count),
            scratch_shapes=[
                pltpu.VMEM((box * leaf, width), F32),
                pltpu.VMEM(proj.shape, F32),
                pltpu.VMEM(col.shape, F32),
                pltpu.VMEM(mid.shape, F32),
                pltpu.VMEM((box * rank, width), BF16),
                pltpu.VMEM((box * rank, width), BF16),
                pltpu.SemaphoreType.DMA((2 * pieces + 2 * levels + 1,)),
            ],
            compiler_params=pltpu.CompilerParams(vmem_limit_bytes=limit * 2**20),
            cost_estimate=cost,
            name="column_side",
        )(right_sides, proj, col, mid)
        return [outs[k * n_seg:(k + 1) * n_seg] for k in range(count)]

    def row_weights():
        return pl.pallas_call(
            weights_kernel,
            in_specs=[in_vmem],
            out_specs=in_vmem,
            out_shape=jax.ShapeDtypeStruct((levels, pairs, 2 * rank, 4 * rank), BF16),
            compiler_params=params,
            cost_estimate=cost,
            name="row_weights",
        )(row)

    def expand_weights(other):
        return pl.pallas_call(
            functools.partial(expand_weights_kernel, n_tile),
            in_specs=[in_vmem] * 2,
            out_specs=in_vmem,
            out_shape=jax.ShapeDtypeStruct((n_tile // 2 * pieces, unit, 4 * rank), BF16),
            compiler_params=params,
            cost_estimate=cost,
            name="expand_weights",
        )(expand, other)

    def row_side(parts, wide):
        return pl.pallas_call(
            functools.partial(row_kernel, n_seg, n_tile, leaf),
            in_specs=[in_vmem] * (n_seg + 1),
            out_specs=[in_vmem] * 4,
            out_shape=[quarter] * 4,
            scratch_shapes=[pltpu.VMEM((box * rank, CHUNK), t) for t in (BF16, BF16, F32)],
            compiler_params=params,
            cost_estimate=pl.CostEstimate(flops=20_000_000_000, bytes_accessed=100_000, transcendentals=0),
            name="row_side",
        )(*parts, wide)

    def expanded(part, own, other, last):
        return pl.pallas_call(
            functools.partial(expand_kernel, part),
            in_specs=[in_vmem] * 3,
            out_specs=in_vmem,
            out_shape=summed,
            compiler_params=params,
            cost_estimate=pl.CostEstimate(flops=(1 - part) * 2_000_000_000 + 1, bytes_accessed=100_000, transcendentals=0),
            name="expand",
        )(own, other, last)

    def swap(x, axis, size, mask):
        return lax.ppermute(x, axis, [(i, i ^ mask) for i in range(size)])

    def exchange(parts, *after):
        return [parts[0]] + [swap(tie(parts[k], *after) if after else parts[k], "seg", n_seg, k) for k in range(1, n_seg)]

    def total(terms, low, high):
        return functools.reduce(jnp.add, [x[low:high] for x in terms])

    def next_send(terms):
        left = terms[-1].shape[0]
        return total(terms, left // 2, left)

    parts = column_side(0, 1, mid, 53)
    received = {0: exchange(parts[0])}
    parts += column_side(1, chunks - 1, tie(mid, parts[0][-1]), 52)
    received[1] = exchange(parts[1])
    wide = row_weights()
    last_wide = expand_weights(swap(tie(expand, parts[-1][0]), "tile", n_tile, 1))

    terms, sends, lows = [], {}, []
    last = chunks - 1

    def forward(c, b, *after):
        terms[c][-1] = tie(terms[c][-1], *after)
        sends[c, b] = next_send(terms[c])
        terms[c].append(swap(sends[c, b], "tile", n_tile, 1 << b))
        return sends[c, b]

    def low_half(c, *after):
        own, other = lows[c]
        terms[c][0] = expanded(0, own, tie(other, *after), last_wide)
        return terms[c][0]

    for c in range(chunks):
        after = sends[c - 1, 1] if c else parts[-1][0]
        own_low, own_high, low, high = row_side([tie(x, after) for x in received[c]], wide)
        lows.append((own_low, swap(low, "tile", n_tile, 1)))
        done = []
        if c >= 1:
            done.append(low_half(c - 1, own_high))
        if c >= 2:
            done.append(forward(c - 2, 2, own_high))
        if c >= 3 and bits > 3:
            done.append(forward(c - 3, 3, own_high))
        got = swap(high, "tile", n_tile, 1)
        if done:
            got = tie(got, *done)
        sends[c, 1] = expanded(1, own_high, got, last_wide)
        terms.append([None, swap(sends[c, 1], "tile", n_tile, 2)])
        if c + 2 < chunks:
            received[c + 2] = exchange(parts[c + 2], sends[c, 1])
    low_half(last, sends[last, 1])
    done = [forward(last - 1, 2, sends[last, 1])]
    if bits > 3:
        done += [forward(k, 3, sends[last, 1]) for k in range(max(0, last - 2), last)]
    forward(last, 2, *done)
    for b in range(3, bits):
        for c in range(chunks):
            if (c, b) not in sends:
                forward(c, b, sends[last, 2])
    for c in range(last):
        terms[c][-1] = tie(terms[c][-1], sends[last, 2])
    return jnp.concatenate([total(t, 0, out_rows) for t in terms], axis=1)


def solution(mesh):
    in_specs = (
        P(("tile", "seg"), None),
        P("tile", "seg", None, None),
        P("tile", None, "seg", None, None),
        P("tile", "seg", None, None),
        P("tile", None, "seg", None, None),
        P("tile", "seg", None, None),
    )
    out_specs = P(("seg", "tile"), None)
    body = functools.partial(shards, mesh.shape["tile"], mesh.shape["seg"])
    return jax.shard_map(body, mesh=mesh, in_specs=in_specs, out_specs=out_specs, check_vma=False)
```

```python
import functools

import jax
import jax.numpy as jnp
from jax import lax
from jax.experimental import pallas as pl
from jax.experimental.pallas import tpu as pltpu
from jax.sharding import PartitionSpec as P

F32 = jnp.float32
BF16 = jnp.bfloat16
CHUNK = 128
FIRST = 52.5
SECOND = 52


def split(x):
    hi = x.astype(BF16)
    return hi, (x - hi.astype(F32)).astype(BF16)


def dot(a, b, dims=((1,), (0,))):
    return lax.dot_general(a, b, (dims, ((), ())), preferred_element_type=F32)


def wide_of(w):
    return jnp.concatenate(split(w), axis=1)


def product3(wide, v_hi, v_lo):
    depth, width = v_hi.shape
    if width > CHUNK:
        return dot(wide, jnp.concatenate([v_hi, v_hi], axis=0)) + dot(wide[:, :depth], v_lo)
    left = jnp.concatenate([v_hi, v_hi], axis=0)
    right = jnp.concatenate([v_lo, jnp.zeros_like(v_lo)], axis=0)
    both = dot(wide, jnp.concatenate([left, right], axis=1))
    return both[:, :width] + both[:, width:]


def pair_of(hi, lo, first, second, rank, cols=slice(None)):
    return [jnp.concatenate([x[pl.ds(first, rank), cols], x[pl.ds(second, rank), cols]], axis=0) for x in (hi, lo)]


def level_step(level, wide_at, hi, lo, rank, cuts):
    d = 2**level
    for j in range(hi.shape[0] // (2 * rank)):
        first = ((j // d) * 2 * d + j % d) * rank
        second = first + d * rank
        wide = wide_at(j)
        for cols in cuts:
            out_hi, out_lo = split(product3(wide, *pair_of(hi, lo, first, second, rank, cols)))
            for place, half in ((first, 0), (second, 1)):
                hi[pl.ds(place, rank), cols] = out_hi[half * rank:(half + 1) * rank]
                lo[pl.ds(place, rank), cols] = out_lo[half * rank:(half + 1) * rank]


def cuts_of(width):
    odd = width % (2 * CHUNK)
    return ([slice(0, odd)] if odd else []) + [slice(k, k + 2 * CHUNK) for k in range(odd, width, 2 * CHUNK)]


def project(n, wide, x, hi, lo, cuts):
    rank, leaf = wide.shape[0], wide.shape[1] // 2
    for cols in cuts:
        c_hi, c_lo = split(product3(wide, *split(x[n * leaf:(n + 1) * leaf, cols])))
        hi[n * rank:(n + 1) * rank, cols] = c_hi
        lo[n * rank:(n + 1) * rank, cols] = c_lo


def middle(n_seg, mid, outs, hi, lo, cuts):
    box, rank = mid.shape[:2]
    share = box // n_seg
    seg = lax.axis_index("seg")
    for delta in reversed(range(n_seg)):
        base = (seg ^ delta) * share
        for p in range(share):
            wide = wide_of(mid[base + p])
            at = pl.multiple_of((base + p) * rank, rank)
            for cols in cuts:
                out = product3(wide, hi[pl.ds(at, rank), cols], lo[pl.ds(at, rank), cols])
                for k in range(out.shape[1] // CHUNK):
                    target = outs[(cols.start // CHUNK + k) * n_seg + delta]
                    target[p * rank:(p + 1) * rank, :] = out[:, k * CHUNK:(k + 1) * CHUNK]


def column_kernel(n_seg, pieces, start, x_hbm, proj_hbm, col_hbm, mid_hbm, *refs):
    outs, (x_ref, proj_ref, col_ref, mid_ref, hi, lo, sems) = refs[:-7], refs[-7:]
    box, rank, leaf = proj_ref.shape
    levels, pairs = col_ref.shape[:2]
    width = x_ref.shape[1]
    per = box // pieces
    copies = []

    def fetch(src, dst):
        copies.append(pltpu.make_async_copy(src, dst, sems.at[len(copies)]))
        copies[-1].start()
        return copies[-1]

    first = []
    for k in range(pieces):
        rows = pl.ds(k * per * leaf, per * leaf)
        leaves = pl.ds(k * per, per)
        first.append((
            fetch(proj_hbm.at[leaves], proj_ref.at[leaves]),
            fetch(x_hbm.at[rows, pl.ds(start, width)], x_ref.at[rows, :]),
        ))
    halves = [pl.ds(k * (pairs // 2), pairs // 2) for k in range(2)]
    cols = [[fetch(col_hbm.at[k, h], col_ref.at[k, h]) for h in halves] for k in range(levels)]
    mid = fetch(mid_hbm, mid_ref)

    cuts = cuts_of(width)
    for k in range(pieces):
        for copy in first[k]:
            copy.wait()
        for n in range(k * per, (k + 1) * per):
            project(n, wide_of(proj_ref[n]), x_ref, hi, lo, cuts)
    for level in range(levels):
        for copy in cols[level]:
            copy.wait()
        level_step(level, lambda j: wide_of(col_ref[level, j]), hi, lo, rank, cuts)
    mid.wait()
    middle(n_seg, mid_ref, outs, hi, lo, cuts)


def slots_of(n_tile, box, leaf):
    bits = n_tile.bit_length() - 1
    out_rows = box * leaf // n_tile
    relative = [int(format(slot, f"0{bits}b")[::-1], 2) for slot in range(n_tile)]
    return relative, out_rows, min(out_rows, leaf), max(1, out_rows // leaf)


def weights_kernel(row_ref, wide_ref):
    for level in range(row_ref.shape[0]):
        for j in range(row_ref.shape[1]):
            wide_ref[level, j] = wide_of(row_ref[level, j])


def expand_weights_kernel(n_tile, exp_ref, other_ref, last_ref):
    box, _, leaf = exp_ref.shape
    tile = lax.axis_index("tile")
    relative, out_rows, unit, pieces = slots_of(n_tile, box, leaf)
    for slot in range(n_tile // 2):
        block = tile ^ relative[slot]
        for piece in range(pieces):
            n = (block * out_rows + piece * unit) // leaf
            both = jnp.concatenate([exp_ref[n], other_ref[n]], axis=0).T
            rows = both[:unit]
            for k in range(1, leaf // unit):
                rows = jnp.where(block % (leaf // unit) == k, both[k * unit:(k + 1) * unit], rows)
            last_ref[slot * pieces + piece] = wide_of(rows)


def row_kernel(n_seg, n_tile, leaf, *refs):
    ins, (row_ref, *outs, hi, lo, full) = refs[:n_seg], refs[n_seg:]
    levels, pairs = row_ref.shape[:2]
    box = 2 * pairs
    rank = hi.shape[0] // box
    share = box // n_seg
    seg = lax.axis_index("seg")
    tile = lax.axis_index("tile")
    for delta in range(n_seg):
        base = (seg ^ delta) * share
        at = pl.multiple_of(base * rank, share * rank)
        v_hi, v_lo = split(ins[delta][...])
        hi[pl.ds(at, share * rank), :] = v_hi
        lo[pl.ds(at, share * rank), :] = v_lo
    for level in range(levels - 1):
        level_step(level, lambda j: row_ref[level, j], hi, lo, rank, [slice(None)])
    for j in range(pairs):
        second = (j + pairs) * rank
        out = product3(row_ref[levels - 1, j], *pair_of(hi, lo, j * rank, second, rank))
        full[j * rank:(j + 1) * rank, :] = out[:rank]
        full[second:second + rank, :] = out[rank:]
    relative, out_rows, unit, pieces = slots_of(n_tile, box, leaf)
    group = n_tile // 4
    for slot in range(n_tile):
        block = tile ^ relative[slot]
        for piece in range(pieces):
            n = (block * out_rows + piece * unit) // leaf
            at = (slot % group * pieces + piece) * rank
            outs[slot // group][at:at + rank, :] = full[pl.ds(pl.multiple_of(n * rank, rank), rank), :]


def expand_kernel(part, own_ref, other_ref, last_ref, out_ref):
    rank = last_ref.shape[2] // 4
    unit = last_ref.shape[1]
    for k in range(own_ref.shape[0] // rank):
        rows = slice(k * rank, (k + 1) * rank)
        v = jnp.concatenate([own_ref[rows, :], other_ref[rows, :]], axis=0)
        wide = last_ref[part * own_ref.shape[0] // rank + k]
        out_ref[k * unit:(k + 1) * unit, :] = product3(wide, *split(v))


def tie(x, *others):
    return lax.optimization_barrier((x, *others))[0]


def shards(n_tile, n_seg, right_sides, leaf_proj, col_levels, middle_factor, row_levels, leaf_expand):
    proj, col, mid, row = leaf_proj[0], col_levels[0], middle_factor[0], row_levels[0]
    expand = jnp.swapaxes(leaf_expand[0], 1, 2)
    box, rank, leaf = proj.shape
    levels, pairs = col.shape[:2]
    chunks = right_sides.shape[1] // CHUNK
    _, out_rows, unit, pieces = slots_of(n_tile, box, leaf)
    bits = n_tile.bit_length() - 1
    part = jax.ShapeDtypeStruct((box * rank // n_seg, CHUNK), F32)
    quarter = jax.ShapeDtypeStruct((n_tile // 4 * pieces * rank, CHUNK), F32)
    summed = jax.ShapeDtypeStruct((box * leaf // 4, CHUNK), F32)
    params = pltpu.CompilerParams(vmem_limit_bytes=16 * 2**20)
    cost = pl.CostEstimate(flops=1_000_000, bytes_accessed=100_000, transcendentals=0)
    in_hbm = pl.BlockSpec(memory_space=pltpu.HBM)
    in_vmem = pl.BlockSpec(memory_space=pltpu.VMEM)

    def column_side(start, count, mid, limit):
        pieces = 4
        width = count * CHUNK
        outs = pl.pallas_call(
            functools.partial(column_kernel, n_seg, pieces, start * CHUNK),
            in_specs=[in_hbm] * 4,
            out_specs=[in_vmem] * (n_seg * count),
            out_shape=[part] * (n_seg * count),
            scratch_shapes=[
                pltpu.VMEM((box * leaf, width), F32),
                pltpu.VMEM(proj.shape, F32),
                pltpu.VMEM(col.shape, F32),
                pltpu.VMEM(mid.shape, F32),
                pltpu.VMEM((box * rank, width), BF16),
                pltpu.VMEM((box * rank, width), BF16),
                pltpu.SemaphoreType.DMA((2 * pieces + 2 * levels + 1,)),
            ],
            compiler_params=pltpu.CompilerParams(vmem_limit_bytes=int(limit * 2**20)),
            cost_estimate=cost,
            name="column_side",
        )(right_sides, proj, col, mid)
        return [outs[k * n_seg:(k + 1) * n_seg] for k in range(count)]

    def row_weights():
        return pl.pallas_call(
            weights_kernel,
            in_specs=[in_vmem],
            out_specs=in_vmem,
            out_shape=jax.ShapeDtypeStruct((levels, pairs, 2 * rank, 4 * rank), BF16),
            compiler_params=params,
            cost_estimate=cost,
            name="row_weights",
        )(row)

    def expand_weights(other):
        return pl.pallas_call(
            functools.partial(expand_weights_kernel, n_tile),
            in_specs=[in_vmem] * 2,
            out_specs=in_vmem,
            out_shape=jax.ShapeDtypeStruct((n_tile // 2 * pieces, unit, 4 * rank), BF16),
            compiler_params=params,
            cost_estimate=cost,
            name="expand_weights",
        )(expand, other)

    def row_side(parts, wide):
        return pl.pallas_call(
            functools.partial(row_kernel, n_seg, n_tile, leaf),
            in_specs=[in_vmem] * (n_seg + 1),
            out_specs=[in_vmem] * 4,
            out_shape=[quarter] * 4,
            scratch_shapes=[pltpu.VMEM((box * rank, CHUNK), t) for t in (BF16, BF16, F32)],
            compiler_params=params,
            cost_estimate=pl.CostEstimate(flops=20_000_000_000, bytes_accessed=100_000, transcendentals=0),
            name="row_side",
        )(*parts, wide)

    def expanded(part, own, other, last):
        return pl.pallas_call(
            functools.partial(expand_kernel, part),
            in_specs=[in_vmem] * 3,
            out_specs=in_vmem,
            out_shape=summed,
            compiler_params=params,
            cost_estimate=pl.CostEstimate(flops=(1 - part) * 2_000_000_000 + 1, bytes_accessed=100_000, transcendentals=0),
            name="expand",
        )(own, other, last)

    def swap(x, axis, size, mask):
        return lax.ppermute(x, axis, [(i, i ^ mask) for i in range(size)])

    def exchange(parts, *after):
        return [parts[0]] + [swap(tie(parts[k], *after) if after else parts[k], "seg", n_seg, k) for k in range(1, n_seg)]

    def total(terms, low, high):
        return functools.reduce(jnp.add, [x[low:high] for x in terms])

    def next_send(terms):
        left = terms[-1].shape[0]
        return total(terms, left // 2, left)

    parts = column_side(0, 2, mid, FIRST)
    received = {0: exchange(parts[0])}
    parts += column_side(2, chunks - 2, tie(mid, parts[0][-1]), SECOND)
    received[1] = exchange(parts[1])
    wide = row_weights()
    last_wide = expand_weights(swap(tie(expand, parts[-1][0]), "tile", n_tile, 1))

    terms, sends, lows = [], {}, []
    last = chunks - 1

    def forward(group, b, *after):
        for c in group:
            terms[c][-1] = tie(terms[c][-1], *after)
        send = jnp.concatenate([next_send(terms[c]) for c in group])
        sends[group[-1], b] = send
        got = swap(send, "tile", n_tile, 1 << b)
        rows = got.shape[0] // len(group)
        for k, c in enumerate(group):
            terms[c].append(got[k * rows:(k + 1) * rows])
        return send

    def low_half(c, *after):
        own, other = lows[c]
        terms[c][0] = expanded(0, own, tie(other, *after), last_wide)
        return terms[c][0]

    early = list(range(last - 1))
    for c in range(chunks):
        after = sends[c - 1, 1] if c else parts[-1][0]
        own_low, own_high, low, high = row_side([tie(x, after) for x in received[c]], wide)
        lows.append((own_low, swap(low, "tile", n_tile, 1)))
        done = []
        if c >= 1:
            done.append(low_half(c - 1, own_high))
        if c == last:
            done.append(forward(early, 2, own_high))
        got = swap(high, "tile", n_tile, 1)
        if done:
            got = tie(got, *done)
        sends[c, 1] = expanded(1, own_high, got, last_wide)
        terms.append([None, swap(sends[c, 1], "tile", n_tile, 2)])
        if c + 2 < chunks:
            received[c + 2] = exchange(parts[c + 2], sends[c, 1])
    low_half(last, sends[last, 1])
    done = [forward([last - 1], 2, sends[last, 1])]
    if bits > 3:
        done += [forward(group, 3, sends[last, 1]) for group in (early, [last - 1])]
    forward([last], 2, *done)
    for b in range(3, bits):
        for group in (early, [last - 1], [last]):
            if (group[-1], b) not in sends:
                forward(group, b, sends[last, 2])
    for c in range(last):
        terms[c][-1] = tie(terms[c][-1], sends[last, 2])
    return jnp.concatenate([total(t, 0, out_rows) for t in terms], axis=1)


def solution(mesh):
    in_specs = (
        P(("tile", "seg"), None),
        P("tile", "seg", None, None),
        P("tile", None, "seg", None, None),
        P("tile", "seg", None, None),
        P("tile", None, "seg", None, None),
        P("tile", "seg", None, None),
    )
    out_specs = P(("seg", "tile"), None)
    body = functools.partial(shards, mesh.shape["tile"], mesh.shape["seg"])
    return jax.shard_map(body, mesh=mesh, in_specs=in_specs, out_specs=out_specs, check_vma=False)
```

```python
import functools

import jax
import jax.numpy as jnp
from jax import lax
from jax.experimental import pallas as pl
from jax.experimental.pallas import tpu as pltpu
from jax.sharding import PartitionSpec as P

F32 = jnp.float32
BF16 = jnp.bfloat16
CHUNK = 128
ROW = 20_000_000_000


def split(x):
    hi = x.astype(BF16)
    return hi, (x - hi.astype(F32)).astype(BF16)


def dot(a, b, dims=((1,), (0,))):
    return lax.dot_general(a, b, (dims, ((), ())), preferred_element_type=F32)


def wide_of(w):
    return jnp.concatenate(split(w), axis=1)


def product3(wide, v_hi, v_lo):
    depth, width = v_hi.shape
    if width > CHUNK:
        return dot(wide, jnp.concatenate([v_hi, v_hi], axis=0)) + dot(wide[:, :depth], v_lo)
    left = jnp.concatenate([v_hi, v_hi], axis=0)
    right = jnp.concatenate([v_lo, jnp.zeros_like(v_lo)], axis=0)
    both = dot(wide, jnp.concatenate([left, right], axis=1))
    return both[:, :width] + both[:, width:]


def pair_of(hi, lo, first, second, rank, cols=slice(None)):
    return [jnp.concatenate([x[pl.ds(first, rank), cols], x[pl.ds(second, rank), cols]], axis=0) for x in (hi, lo)]


def level_step(level, wide_at, hi, lo, rank, cuts):
    d = 2**level
    for j in range(hi.shape[0] // (2 * rank)):
        first = ((j // d) * 2 * d + j % d) * rank
        second = first + d * rank
        wide = wide_at(j)
        for cols in cuts:
            out_hi, out_lo = split(product3(wide, *pair_of(hi, lo, first, second, rank, cols)))
            for place, half in ((first, 0), (second, 1)):
                hi[pl.ds(place, rank), cols] = out_hi[half * rank:(half + 1) * rank]
                lo[pl.ds(place, rank), cols] = out_lo[half * rank:(half + 1) * rank]


def cuts_of(width):
    odd = width % (2 * CHUNK)
    return ([slice(0, odd)] if odd else []) + [slice(k, k + 2 * CHUNK) for k in range(odd, width, 2 * CHUNK)]


def project(n, wide, x, hi, lo, cuts):
    rank, leaf = wide.shape[0], wide.shape[1] // 2
    for cols in cuts:
        c_hi, c_lo = split(product3(wide, *split(x[n * leaf:(n + 1) * leaf, cols])))
        hi[n * rank:(n + 1) * rank, cols] = c_hi
        lo[n * rank:(n + 1) * rank, cols] = c_lo


def middle(n_seg, mid, outs, hi, lo, cuts):
    box, rank = mid.shape[:2]
    share = box // n_seg
    seg = lax.axis_index("seg")
    for delta in reversed(range(n_seg)):
        base = (seg ^ delta) * share
        for p in range(share):
            wide = wide_of(mid[base + p])
            at = pl.multiple_of((base + p) * rank, rank)
            for cols in cuts:
                out = product3(wide, hi[pl.ds(at, rank), cols], lo[pl.ds(at, rank), cols])
                for k in range(out.shape[1] // CHUNK):
                    target = outs[(cols.start // CHUNK + k) * n_seg + delta]
                    target[p * rank:(p + 1) * rank, :] = out[:, k * CHUNK:(k + 1) * CHUNK]


def column_kernel(n_seg, pieces, start, x_hbm, proj_hbm, col_hbm, mid_hbm, *refs):
    outs, (x_ref, proj_ref, col_ref, mid_ref, hi, lo, sems) = refs[:-7], refs[-7:]
    box, rank, leaf = proj_ref.shape
    levels, pairs = col_ref.shape[:2]
    width = x_ref.shape[1]
    per = box // pieces
    copies = []

    def fetch(src, dst):
        copies.append(pltpu.make_async_copy(src, dst, sems.at[len(copies)]))
        copies[-1].start()
        return copies[-1]

    first = []
    for k in range(pieces):
        rows = pl.ds(k * per * leaf, per * leaf)
        leaves = pl.ds(k * per, per)
        first.append((
            fetch(proj_hbm.at[leaves], proj_ref.at[leaves]),
            fetch(x_hbm.at[rows, pl.ds(start, width)], x_ref.at[rows, :]),
        ))
    halves = [pl.ds(k * (pairs // 2), pairs // 2) for k in range(2)]
    cols = [[fetch(col_hbm.at[k, h], col_ref.at[k, h]) for h in halves] for k in range(levels)]
    mid = fetch(mid_hbm, mid_ref)

    cuts = cuts_of(width)
    for k in range(pieces):
        for copy in first[k]:
            copy.wait()
        for n in range(k * per, (k + 1) * per):
            project(n, wide_of(proj_ref[n]), x_ref, hi, lo, cuts)
    for level in range(levels):
        for copy in cols[level]:
            copy.wait()
        level_step(level, lambda j: wide_of(col_ref[level, j]), hi, lo, rank, cuts)
    mid.wait()
    middle(n_seg, mid_ref, outs, hi, lo, cuts)


def slots_of(n_tile, box, leaf):
    bits = n_tile.bit_length() - 1
    out_rows = box * leaf // n_tile
    relative = [int(format(slot, f"0{bits}b")[::-1], 2) for slot in range(n_tile)]
    return relative, out_rows, min(out_rows, leaf), max(1, out_rows // leaf)


def weights_kernel(row_ref, wide_ref):
    for level in range(row_ref.shape[0]):
        for j in range(row_ref.shape[1]):
            wide_ref[level, j] = wide_of(row_ref[level, j])


def expand_weights_kernel(n_tile, exp_ref, other_ref, last_ref):
    box, _, leaf = exp_ref.shape
    tile = lax.axis_index("tile")
    relative, out_rows, unit, pieces = slots_of(n_tile, box, leaf)
    for slot in range(n_tile // 2):
        block = tile ^ relative[slot]
        for piece in range(pieces):
            n = (block * out_rows + piece * unit) // leaf
            both = jnp.concatenate([exp_ref[n], other_ref[n]], axis=0).T
            rows = both[:unit]
            for k in range(1, leaf // unit):
                rows = jnp.where(block % (leaf // unit) == k, both[k * unit:(k + 1) * unit], rows)
            last_ref[slot * pieces + piece] = wide_of(rows)


def row_kernel(n_seg, n_tile, leaf, *refs):
    ins, (row_ref, *outs, hi, lo, full) = refs[:n_seg], refs[n_seg:]
    levels, pairs = row_ref.shape[:2]
    box = 2 * pairs
    rank = hi.shape[0] // box
    share = box // n_seg
    seg = lax.axis_index("seg")
    tile = lax.axis_index("tile")
    for delta in range(n_seg):
        base = (seg ^ delta) * share
        at = pl.multiple_of(base * rank, share * rank)
        v_hi, v_lo = split(ins[delta][...])
        hi[pl.ds(at, share * rank), :] = v_hi
        lo[pl.ds(at, share * rank), :] = v_lo
    for level in range(levels - 1):
        level_step(level, lambda j: row_ref[level, j], hi, lo, rank, [slice(None)])
    for j in range(pairs):
        second = (j + pairs) * rank
        out = product3(row_ref[levels - 1, j], *pair_of(hi, lo, j * rank, second, rank))
        full[j * rank:(j + 1) * rank, :] = out[:rank]
        full[second:second + rank, :] = out[rank:]
    relative, out_rows, unit, pieces = slots_of(n_tile, box, leaf)
    group = n_tile // 4
    for slot in range(n_tile):
        block = tile ^ relative[slot]
        for piece in range(pieces):
            n = (block * out_rows + piece * unit) // leaf
            at = (slot % group * pieces + piece) * rank
            outs[slot // group][at:at + rank, :] = full[pl.ds(pl.multiple_of(n * rank, rank), rank), :]


def expand_kernel(part, own_ref, other_ref, last_ref, out_ref):
    rank = last_ref.shape[2] // 4
    unit = last_ref.shape[1]
    for k in range(own_ref.shape[0] // rank):
        rows = slice(k * rank, (k + 1) * rank)
        v = jnp.concatenate([own_ref[rows, :], other_ref[rows, :]], axis=0)
        wide = last_ref[part * own_ref.shape[0] // rank + k]
        out_ref[k * unit:(k + 1) * unit, :] = product3(wide, *split(v))


def tie(x, *others):
    return lax.optimization_barrier((x, *others))[0]


def shards(n_tile, n_seg, right_sides, leaf_proj, col_levels, middle_factor, row_levels, leaf_expand):
    proj, col, mid, row = leaf_proj[0], col_levels[0], middle_factor[0], row_levels[0]
    expand = jnp.swapaxes(leaf_expand[0], 1, 2)
    box, rank, leaf = proj.shape
    levels, pairs = col.shape[:2]
    chunks = right_sides.shape[1] // CHUNK
    _, out_rows, unit, pieces = slots_of(n_tile, box, leaf)
    bits = n_tile.bit_length() - 1
    part = jax.ShapeDtypeStruct((box * rank // n_seg, CHUNK), F32)
    quarter = jax.ShapeDtypeStruct((n_tile // 4 * pieces * rank, CHUNK), F32)
    summed = jax.ShapeDtypeStruct((box * leaf // 4, CHUNK), F32)
    params = pltpu.CompilerParams(vmem_limit_bytes=16 * 2**20)
    cost = pl.CostEstimate(flops=1_000_000, bytes_accessed=100_000, transcendentals=0)
    in_hbm = pl.BlockSpec(memory_space=pltpu.HBM)
    in_vmem = pl.BlockSpec(memory_space=pltpu.VMEM)

    def column_side(start, count, mid, limit):
        pieces = 4
        width = count * CHUNK
        outs = pl.pallas_call(
            functools.partial(column_kernel, n_seg, pieces, start * CHUNK),
            in_specs=[in_hbm] * 4,
            out_specs=[in_vmem] * (n_seg * count),
            out_shape=[part] * (n_seg * count),
            scratch_shapes=[
                pltpu.VMEM((box * leaf, width), F32),
                pltpu.VMEM(proj.shape, F32),
                pltpu.VMEM(col.shape, F32),
                pltpu.VMEM(mid.shape, F32),
                pltpu.VMEM((box * rank, width), BF16),
                pltpu.VMEM((box * rank, width), BF16),
                pltpu.SemaphoreType.DMA((2 * pieces + 2 * levels + 1,)),
            ],
            compiler_params=pltpu.CompilerParams(vmem_limit_bytes=limit * 2**20),
            cost_estimate=cost,
            name="column_side",
        )(right_sides, proj, col, mid)
        return [outs[k * n_seg:(k + 1) * n_seg] for k in range(count)]

    def row_weights():
        return pl.pallas_call(
            weights_kernel,
            in_specs=[in_vmem],
            out_specs=in_vmem,
            out_shape=jax.ShapeDtypeStruct((levels, pairs, 2 * rank, 4 * rank), BF16),
            compiler_params=params,
            cost_estimate=cost,
            name="row_weights",
        )(row)

    def expand_weights(other):
        return pl.pallas_call(
            functools.partial(expand_weights_kernel, n_tile),
            in_specs=[in_vmem] * 2,
            out_specs=in_vmem,
            out_shape=jax.ShapeDtypeStruct((n_tile // 2 * pieces, unit, 4 * rank), BF16),
            compiler_params=params,
            cost_estimate=cost,
            name="expand_weights",
        )(expand, other)

    def row_side(parts, wide):
        return pl.pallas_call(
            functools.partial(row_kernel, n_seg, n_tile, leaf),
            in_specs=[in_vmem] * (n_seg + 1),
            out_specs=[in_vmem] * 4,
            out_shape=[quarter] * 4,
            scratch_shapes=[pltpu.VMEM((box * rank, CHUNK), t) for t in (BF16, BF16, F32)],
            compiler_params=params,
            cost_estimate=pl.CostEstimate(flops=ROW, bytes_accessed=100_000, transcendentals=0),
            name="row_side",
        )(*parts, wide)

    def expanded(part, own, other, last):
        return pl.pallas_call(
            functools.partial(expand_kernel, part),
            in_specs=[in_vmem] * 3,
            out_specs=in_vmem,
            out_shape=summed,
            compiler_params=params,
            cost_estimate=pl.CostEstimate(flops=(1 - part) * 2_000_000_000 + 1, bytes_accessed=100_000, transcendentals=0),
            name="expand",
        )(own, other, last)

    def swap(x, axis, size, mask):
        return lax.ppermute(x, axis, [(i, i ^ mask) for i in range(size)])

    def exchange(parts, *after):
        return [parts[0]] + [swap(tie(parts[k], *after) if after else parts[k], "seg", n_seg, k) for k in range(1, n_seg)]

    def total(terms, low, high):
        return functools.reduce(jnp.add, [x[low:high] for x in terms])

    def next_send(terms):
        left = terms[-1].shape[0]
        return total(terms, left // 2, left)

    parts = column_side(0, 1, mid, 53)
    received = {0: exchange(parts[0])}
    parts += column_side(1, chunks - 1, tie(mid, parts[0][-1]), 52)
    received[1] = exchange(parts[1])
    wide = row_weights()
    last_wide = expand_weights(swap(tie(expand, wide), "tile", n_tile, 1))

    terms, sends, lows = [], {}, []
    last = chunks - 1

    def forward(group, b, *after):
        for c in group:
            terms[c][-1] = tie(terms[c][-1], *after)
        send = jnp.concatenate([next_send(terms[c]) for c in group])
        sends[group[-1], b] = send
        got = swap(send, "tile", n_tile, 1 << b)
        rows = got.shape[0] // len(group)
        for k, c in enumerate(group):
            terms[c].append(got[k * rows:(k + 1) * rows])
        return send

    def low_half(c, *after):
        own, other = lows[c]
        terms[c][0] = expanded(0, own, tie(other, *after), last_wide)
        return terms[c][0]

    early = list(range(last - 1))
    for c in range(chunks):
        after = [sends[c - 1, 1]] if c else [parts[-1][0]]
        if c == last:
            after.append(forward(early, 2, sends[c - 1, 1]))
        own_low, own_high, low, high = row_side([tie(x, *after) for x in received[c]], wide)
        lows.append((own_low, swap(low, "tile", n_tile, 1)))
        done = []
        if c >= 1:
            done.append(low_half(c - 1, own_high))
        got = swap(high, "tile", n_tile, 1)
        if done:
            got = tie(got, *done)
        sends[c, 1] = expanded(1, own_high, got, last_wide)
        terms.append([None, swap(sends[c, 1], "tile", n_tile, 2)])
        if c + 2 < chunks:
            received[c + 2] = exchange(parts[c + 2], own_high)
    low_half(last, sends[last, 1])
    done = sends[last, 1]
    for group, b in ((early, 3), ([last - 1], 2), ([last], 2), ([last - 1], 3), ([last], 3)):
        if b < bits:
            done = forward(group, b, done)
    for b in range(4, bits):
        for group in (early, [last - 1], [last]):
            done = forward(group, b, done)
    return jnp.concatenate([total(t, 0, out_rows) for t in terms], axis=1)


def solution(mesh):
    in_specs = (
        P(("tile", "seg"), None),
        P("tile", "seg", None, None),
        P("tile", None, "seg", None, None),
        P("tile", "seg", None, None),
        P("tile", None, "seg", None, None),
        P("tile", "seg", None, None),
    )
    out_specs = P(("seg", "tile"), None)
    body = functools.partial(shards, mesh.shape["tile"], mesh.shape["seg"])
    return jax.shard_map(body, mesh=mesh, in_specs=in_specs, out_specs=out_specs, check_vma=False)
```

```python
import functools

import jax
import jax.numpy as jnp
from jax import lax
from jax.experimental import pallas as pl
from jax.experimental.pallas import tpu as pltpu
from jax.sharding import PartitionSpec as P

F32 = jnp.float32
BF16 = jnp.bfloat16
CHUNK = 128
ROW = 20_000_000_000
LOW = 1


def split(x):
    hi = x.astype(BF16)
    return hi, (x - hi.astype(F32)).astype(BF16)


def dot(a, b, dims=((1,), (0,))):
    return lax.dot_general(a, b, (dims, ((), ())), preferred_element_type=F32)


def wide_of(w):
    return jnp.concatenate(split(w), axis=1)


def product3(wide, v_hi, v_lo):
    depth, width = v_hi.shape
    if width > CHUNK:
        return dot(wide, jnp.concatenate([v_hi, v_hi], axis=0)) + dot(wide[:, :depth], v_lo)
    left = jnp.concatenate([v_hi, v_hi], axis=0)
    right = jnp.concatenate([v_lo, jnp.zeros_like(v_lo)], axis=0)
    both = dot(wide, jnp.concatenate([left, right], axis=1))
    return both[:, :width] + both[:, width:]


def pair_of(hi, lo, first, second, rank, cols=slice(None)):
    return [jnp.concatenate([x[pl.ds(first, rank), cols], x[pl.ds(second, rank), cols]], axis=0) for x in (hi, lo)]


def level_step(level, wide_at, hi, lo, rank, cuts):
    d = 2**level
    for j in range(hi.shape[0] // (2 * rank)):
        first = ((j // d) * 2 * d + j % d) * rank
        second = first + d * rank
        wide = wide_at(j)
        for cols in cuts:
            out_hi, out_lo = split(product3(wide, *pair_of(hi, lo, first, second, rank, cols)))
            for place, half in ((first, 0), (second, 1)):
                hi[pl.ds(place, rank), cols] = out_hi[half * rank:(half + 1) * rank]
                lo[pl.ds(place, rank), cols] = out_lo[half * rank:(half + 1) * rank]


def cuts_of(width):
    odd = width % (2 * CHUNK)
    return ([slice(0, odd)] if odd else []) + [slice(k, k + 2 * CHUNK) for k in range(odd, width, 2 * CHUNK)]


def project(n, wide, x, hi, lo, cuts):
    rank, leaf = wide.shape[0], wide.shape[1] // 2
    for cols in cuts:
        c_hi, c_lo = split(product3(wide, *split(x[n * leaf:(n + 1) * leaf, cols])))
        hi[n * rank:(n + 1) * rank, cols] = c_hi
        lo[n * rank:(n + 1) * rank, cols] = c_lo


def middle(n_seg, mid, outs, hi, lo, cuts):
    box, rank = mid.shape[:2]
    share = box // n_seg
    seg = lax.axis_index("seg")
    for delta in reversed(range(n_seg)):
        base = (seg ^ delta) * share
        for p in range(share):
            wide = wide_of(mid[base + p])
            at = pl.multiple_of((base + p) * rank, rank)
            for cols in cuts:
                out = product3(wide, hi[pl.ds(at, rank), cols], lo[pl.ds(at, rank), cols])
                for k in range(out.shape[1] // CHUNK):
                    target = outs[(cols.start // CHUNK + k) * n_seg + delta]
                    target[p * rank:(p + 1) * rank, :] = out[:, k * CHUNK:(k + 1) * CHUNK]


def column_kernel(n_seg, pieces, start, x_hbm, proj_hbm, col_hbm, mid_hbm, *refs):
    outs, (x_ref, proj_ref, col_ref, mid_ref, hi, lo, sems) = refs[:-7], refs[-7:]
    box, rank, leaf = proj_ref.shape
    levels, pairs = col_ref.shape[:2]
    width = x_ref.shape[1]
    per = box // pieces
    copies = []

    def fetch(src, dst):
        copies.append(pltpu.make_async_copy(src, dst, sems.at[len(copies)]))
        copies[-1].start()
        return copies[-1]

    first = []
    for k in range(pieces):
        rows = pl.ds(k * per * leaf, per * leaf)
        leaves = pl.ds(k * per, per)
        first.append((
            fetch(proj_hbm.at[leaves], proj_ref.at[leaves]),
            fetch(x_hbm.at[rows, pl.ds(start, width)], x_ref.at[rows, :]),
        ))
    halves = [pl.ds(k * (pairs // 2), pairs // 2) for k in range(2)]
    cols = [[fetch(col_hbm.at[k, h], col_ref.at[k, h]) for h in halves] for k in range(levels)]
    mid = fetch(mid_hbm, mid_ref)

    cuts = cuts_of(width)
    for k in range(pieces):
        for copy in first[k]:
            copy.wait()
        for n in range(k * per, (k + 1) * per):
            project(n, wide_of(proj_ref[n]), x_ref, hi, lo, cuts)
    for level in range(levels):
        for copy in cols[level]:
            copy.wait()
        level_step(level, lambda j: wide_of(col_ref[level, j]), hi, lo, rank, cuts)
    mid.wait()
    middle(n_seg, mid_ref, outs, hi, lo, cuts)


def slots_of(n_tile, box, leaf):
    bits = n_tile.bit_length() - 1
    out_rows = box * leaf // n_tile
    relative = [int(format(slot, f"0{bits}b")[::-1], 2) for slot in range(n_tile)]
    return relative, out_rows, min(out_rows, leaf), max(1, out_rows // leaf)


def weights_kernel(n_tile, row_ref, exp_ref, wide_ref, *picks):
    for level in range(row_ref.shape[0]):
        for j in range(row_ref.shape[1]):
            wide_ref[level, j] = wide_of(row_ref[level, j])
    box, _, leaf = exp_ref.shape
    tile = lax.axis_index("tile")
    relative, out_rows, unit, pieces = slots_of(n_tile, box, leaf)
    group = n_tile // 4
    for slot in range(n_tile):
        block = tile ^ relative[slot]
        for piece in range(pieces):
            n = (block * out_rows + piece * unit) // leaf
            picks[slot // group][slot % group * pieces + piece] = exp_ref[n]


def expand_weights_kernel(n_tile, *refs):
    ins, last_ref = refs[:-1], refs[-1]
    count, _, leaf = ins[0].shape
    unit = last_ref.shape[2]
    tile = lax.axis_index("tile")
    relative = slots_of(n_tile, 1, leaf)[0]
    for k in range(count):
        block = tile ^ relative[k * n_tile // 4 // count]
        for part in range(2):
            both = jnp.concatenate([ins[2 * part][k], ins[2 * part + 1][k]], axis=0).T
            rows = both[:unit]
            for at in range(1, leaf // unit):
                rows = jnp.where(block % (leaf // unit) == at, both[at * unit:(at + 1) * unit], rows)
            last_ref[part, k] = wide_of(rows)


def row_kernel(n_seg, n_tile, leaf, *refs):
    ins, (row_ref, *outs, hi, lo, full) = refs[:n_seg], refs[n_seg:]
    levels, pairs = row_ref.shape[:2]
    box = 2 * pairs
    rank = hi.shape[0] // box
    share = box // n_seg
    seg = lax.axis_index("seg")
    tile = lax.axis_index("tile")
    for delta in range(n_seg):
        base = (seg ^ delta) * share
        at = pl.multiple_of(base * rank, share * rank)
        v_hi, v_lo = split(ins[delta][...])
        hi[pl.ds(at, share * rank), :] = v_hi
        lo[pl.ds(at, share * rank), :] = v_lo
    for level in range(levels - 1):
        level_step(level, lambda j: row_ref[level, j], hi, lo, rank, [slice(None)])
    for j in range(pairs):
        second = (j + pairs) * rank
        out = product3(row_ref[levels - 1, j], *pair_of(hi, lo, j * rank, second, rank))
        full[j * rank:(j + 1) * rank, :] = out[:rank]
        full[second:second + rank, :] = out[rank:]
    relative, out_rows, unit, pieces = slots_of(n_tile, box, leaf)
    group = n_tile // 4
    for slot in range(n_tile):
        block = tile ^ relative[slot]
        for piece in range(pieces):
            n = (block * out_rows + piece * unit) // leaf
            at = (slot % group * pieces + piece) * rank
            outs[slot // group][at:at + rank, :] = full[pl.ds(pl.multiple_of(n * rank, rank), rank), :]


def expand_kernel(part, *refs):
    own_ref, other_ref, last_ref = refs[part:part + 3]
    outs = refs[part + 3:]
    count, unit = last_ref.shape[1:3]
    rank = last_ref.shape[3] // 4
    for k in range(count):
        rows = slice(k * rank, (k + 1) * rank)
        v = jnp.concatenate([own_ref[rows, :], other_ref[rows, :]], axis=0)
        out = product3(last_ref[part, k], *split(v))
        if part:
            out = out + refs[0][k * unit:(k + 1) * unit, :]
        at = k * unit * len(outs)
        target, at = outs[at // (count * unit)], at % (count * unit) // len(outs)
        target[at:at + unit, :] = out


def tie(x, *others):
    return lax.optimization_barrier((x, *others))[0]


def shards(n_tile, n_seg, right_sides, leaf_proj, col_levels, middle_factor, row_levels, leaf_expand):
    proj, col, mid, row = leaf_proj[0], col_levels[0], middle_factor[0], row_levels[0]
    expand = jnp.swapaxes(leaf_expand[0], 1, 2)
    box, rank, leaf = proj.shape
    levels, pairs = col.shape[:2]
    chunks = right_sides.shape[1] // CHUNK
    _, out_rows, unit, pieces = slots_of(n_tile, box, leaf)
    bits = n_tile.bit_length() - 1
    part = jax.ShapeDtypeStruct((box * rank // n_seg, CHUNK), F32)
    quarter = jax.ShapeDtypeStruct((n_tile // 4 * pieces * rank, CHUNK), F32)
    eighth = jax.ShapeDtypeStruct((box * leaf // 8, CHUNK), F32)
    summed = jax.ShapeDtypeStruct((box * leaf // 4, CHUNK), F32)
    params = pltpu.CompilerParams(vmem_limit_bytes=16 * 2**20)
    cost = pl.CostEstimate(flops=1_000_000, bytes_accessed=100_000, transcendentals=0)
    in_hbm = pl.BlockSpec(memory_space=pltpu.HBM)
    in_vmem = pl.BlockSpec(memory_space=pltpu.VMEM)

    def column_side(start, count, mid, limit):
        pieces = 4
        width = count * CHUNK
        outs = pl.pallas_call(
            functools.partial(column_kernel, n_seg, pieces, start * CHUNK),
            in_specs=[in_hbm] * 4,
            out_specs=[in_vmem] * (n_seg * count),
            out_shape=[part] * (n_seg * count),
            scratch_shapes=[
                pltpu.VMEM((box * leaf, width), F32),
                pltpu.VMEM(proj.shape, F32),
                pltpu.VMEM(col.shape, F32),
                pltpu.VMEM(mid.shape, F32),
                pltpu.VMEM((box * rank, width), BF16),
                pltpu.VMEM((box * rank, width), BF16),
                pltpu.SemaphoreType.DMA((2 * pieces + 2 * levels + 1,)),
            ],
            compiler_params=pltpu.CompilerParams(vmem_limit_bytes=limit * 2**20),
            cost_estimate=cost,
            name="column_side",
        )(right_sides, proj, col, mid)
        return [outs[k * n_seg:(k + 1) * n_seg] for k in range(count)]

    def row_weights():
        pick = jax.ShapeDtypeStruct((n_tile // 4 * pieces, rank, leaf), F32)
        return pl.pallas_call(
            functools.partial(weights_kernel, n_tile),
            in_specs=[in_vmem] * 2,
            out_specs=[in_vmem] * 5,
            out_shape=[jax.ShapeDtypeStruct((levels, pairs, 2 * rank, 4 * rank), BF16)] + [pick] * 4,
            compiler_params=params,
            cost_estimate=cost,
            name="row_weights",
        )(row, expand)

    def expand_weights(*tiles):
        return pl.pallas_call(
            functools.partial(expand_weights_kernel, n_tile),
            in_specs=[in_vmem] * 4,
            out_specs=in_vmem,
            out_shape=jax.ShapeDtypeStruct((2, n_tile // 4 * pieces, unit, 4 * rank), BF16),
            compiler_params=params,
            cost_estimate=cost,
            name="expand_weights",
        )(*tiles)

    def row_side(parts, wide):
        return pl.pallas_call(
            functools.partial(row_kernel, n_seg, n_tile, leaf),
            in_specs=[in_vmem] * (n_seg + 1),
            out_specs=[in_vmem] * 4,
            out_shape=[quarter] * 4,
            scratch_shapes=[pltpu.VMEM((box * rank, CHUNK), t) for t in (BF16, BF16, F32)],
            compiler_params=params,
            cost_estimate=pl.CostEstimate(flops=ROW, bytes_accessed=100_000, transcendentals=0),
            name="row_side",
        )(*parts, wide)

    def expanded(part, *operands):
        return pl.pallas_call(
            functools.partial(expand_kernel, part),
            in_specs=[in_vmem] * (3 + part),
            out_specs=[in_vmem] * (1 + part),
            out_shape=[eighth] * 2 if part else [summed],
            compiler_params=params,
            cost_estimate=pl.CostEstimate(flops=LOW, bytes_accessed=100_000, transcendentals=0),
            name="expand",
        )(*operands)

    def swap(x, axis, size, mask):
        return lax.ppermute(x, axis, [(i, i ^ mask) for i in range(size)])

    def exchange(parts, *after):
        return [parts[0]] + [swap(tie(parts[k], *after) if after else parts[k], "seg", n_seg, k) for k in range(1, n_seg)]

    def total(terms, low, high):
        return functools.reduce(jnp.add, [x[low:high] for x in terms])

    def next_send(terms):
        left = terms[-1].shape[0]
        return total(terms, left // 2, left)

    parts = column_side(0, 1, mid, 53)
    received = {0: exchange(parts[0])}
    parts += column_side(1, chunks - 1, tie(mid, parts[0][-1]), 52)
    received[1] = exchange(parts[1])
    wide, *picks = row_weights()
    last_wide = expand_weights(picks[0], *[swap(picks[k], "tile", n_tile, m) for k, m in ((2, 1), (1, 2), (3, 3))])

    terms, sends = [], {}
    last = chunks - 1

    def forward(c, b, *after):
        if b == 2:
            near, own, other = terms[c]
            low, send = expanded(1, near, tie(own, *after), other, last_wide)
            terms[c] = [low]
        else:
            terms[c][-1] = tie(terms[c][-1], *after)
            send = next_send(terms[c])
        sends[c, b] = send
        terms[c].append(swap(send, "tile", n_tile, 1 << b))
        return send

    for c in range(chunks):
        after = terms[c - 1][0] if c else parts[-1][0]
        own, to_y, to_core, to_both = row_side([tie(x, after) for x in received[c]], wide)
        from_core = swap(to_core, "tile", n_tile, 1)
        if c:
            from_core = tie(from_core, forward(c - 1, 2, own))
        near = expanded(0, own, from_core, last_wide)[0]
        terms.append([near, swap(to_y, "tile", n_tile, 2), swap(to_both, "tile", n_tile, 3)])
        if c + 2 < chunks:
            received[c + 2] = exchange(parts[c + 2], own)
    done = terms[last][0]
    for c, b in [(k, 3) for k in range(last - 1)] + [(last, 2), (last - 1, 3), (last, 3)]:
        if b < bits:
            done = forward(c, b, done)
    for b in range(4, bits):
        for c in range(chunks):
            done = forward(c, b, done)
    return jnp.concatenate([total(t, 0, out_rows) for t in terms], axis=1)


def solution(mesh):
    in_specs = (
        P(("tile", "seg"), None),
        P("tile", "seg", None, None),
        P("tile", None, "seg", None, None),
        P("tile", "seg", None, None),
        P("tile", None, "seg", None, None),
        P("tile", "seg", None, None),
    )
    out_specs = P(("seg", "tile"), None)
    body = functools.partial(shards, mesh.shape["tile"], mesh.shape["seg"])
    return jax.shard_map(body, mesh=mesh, in_specs=in_specs, out_specs=out_specs, check_vma=False)
```

```python
import functools

import jax
import jax.numpy as jnp
from jax import lax
from jax.experimental import pallas as pl
from jax.experimental.pallas import tpu as pltpu
from jax.sharding import PartitionSpec as P

F32 = jnp.float32
BF16 = jnp.bfloat16
CHUNK = 128
ROW = 20_000_000_000


def split(x):
    hi = x.astype(BF16)
    return hi, (x - hi.astype(F32)).astype(BF16)


def dot(a, b, dims=((1,), (0,))):
    return lax.dot_general(a, b, (dims, ((), ())), preferred_element_type=F32)


def wide_of(w):
    return jnp.concatenate(split(w), axis=1)


def product3(wide, v_hi, v_lo):
    depth, width = v_hi.shape
    if width > CHUNK:
        return dot(wide, jnp.concatenate([v_hi, v_hi], axis=0)) + dot(wide[:, :depth], v_lo)
    left = jnp.concatenate([v_hi, v_hi], axis=0)
    right = jnp.concatenate([v_lo, jnp.zeros_like(v_lo)], axis=0)
    both = dot(wide, jnp.concatenate([left, right], axis=1))
    return both[:, :width] + both[:, width:]


def pair_of(hi, lo, first, second, rank, cols=slice(None)):
    return [jnp.concatenate([x[pl.ds(first, rank), cols], x[pl.ds(second, rank), cols]], axis=0) for x in (hi, lo)]


def level_step(level, wide_at, hi, lo, rank, cuts):
    d = 2**level
    for j in range(hi.shape[0] // (2 * rank)):
        first = ((j // d) * 2 * d + j % d) * rank
        second = first + d * rank
        wide = wide_at(j)
        for cols in cuts:
            out_hi, out_lo = split(product3(wide, *pair_of(hi, lo, first, second, rank, cols)))
            for place, half in ((first, 0), (second, 1)):
                hi[pl.ds(place, rank), cols] = out_hi[half * rank:(half + 1) * rank]
                lo[pl.ds(place, rank), cols] = out_lo[half * rank:(half + 1) * rank]


def cuts_of(width):
    odd = width % (2 * CHUNK)
    return ([slice(0, odd)] if odd else []) + [slice(k, k + 2 * CHUNK) for k in range(odd, width, 2 * CHUNK)]


def project(n, wide, x, hi, lo, cuts):
    rank, leaf = wide.shape[0], wide.shape[1] // 2
    for cols in cuts:
        c_hi, c_lo = split(product3(wide, *split(x[n * leaf:(n + 1) * leaf, cols])))
        hi[n * rank:(n + 1) * rank, cols] = c_hi
        lo[n * rank:(n + 1) * rank, cols] = c_lo


def middle(n_seg, mid, outs, hi, lo, cuts):
    box, rank = mid.shape[:2]
    share = box // n_seg
    seg = lax.axis_index("seg")
    for delta in reversed(range(n_seg)):
        base = (seg ^ delta) * share
        for p in range(share):
            wide = wide_of(mid[base + p])
            at = pl.multiple_of((base + p) * rank, rank)
            for cols in cuts:
                out = product3(wide, hi[pl.ds(at, rank), cols], lo[pl.ds(at, rank), cols])
                for k in range(out.shape[1] // CHUNK):
                    target = outs[(cols.start // CHUNK + k) * n_seg + delta]
                    target[p * rank:(p + 1) * rank, :] = out[:, k * CHUNK:(k + 1) * CHUNK]


def column_kernel(n_seg, pieces, start, x_hbm, proj_hbm, col_hbm, mid_hbm, *refs):
    outs, (x_ref, proj_ref, col_ref, mid_ref, hi, lo, sems) = refs[:-7], refs[-7:]
    box, rank, leaf = proj_ref.shape
    levels, pairs = col_ref.shape[:2]
    width = x_ref.shape[1]
    per = box // pieces
    copies = []

    def fetch(src, dst):
        copies.append(pltpu.make_async_copy(src, dst, sems.at[len(copies)]))
        copies[-1].start()
        return copies[-1]

    first = []
    for k in range(pieces):
        rows = pl.ds(k * per * leaf, per * leaf)
        leaves = pl.ds(k * per, per)
        first.append((
            fetch(proj_hbm.at[leaves], proj_ref.at[leaves]),
            fetch(x_hbm.at[rows, pl.ds(start, width)], x_ref.at[rows, :]),
        ))
    halves = [pl.ds(k * (pairs // 2), pairs // 2) for k in range(2)]
    cols = [[fetch(col_hbm.at[k, h], col_ref.at[k, h]) for h in halves] for k in range(levels)]
    mid = fetch(mid_hbm, mid_ref)

    cuts = cuts_of(width)
    for k in range(pieces):
        for copy in first[k]:
            copy.wait()
        for n in range(k * per, (k + 1) * per):
            project(n, wide_of(proj_ref[n]), x_ref, hi, lo, cuts)
    for level in range(levels):
        for copy in cols[level]:
            copy.wait()
        level_step(level, lambda j: wide_of(col_ref[level, j]), hi, lo, rank, cuts)
    mid.wait()
    middle(n_seg, mid_ref, outs, hi, lo, cuts)


def slots_of(n_tile, box, leaf):
    bits = n_tile.bit_length() - 1
    out_rows = box * leaf // n_tile
    relative = [int(format(slot, f"0{bits}b")[::-1], 2) for slot in range(n_tile)]
    return relative, out_rows, min(out_rows, leaf), max(1, out_rows // leaf)


def weights_kernel(row_ref, exp_ref, wide_ref, out_ref):
    out_ref[...] = exp_ref[...]
    for level in range(row_ref.shape[0]):
        for j in range(row_ref.shape[1]):
            wide_ref[level, j] = wide_of(row_ref[level, j])


def expand_weights_kernel(n_tile, exp_ref, other_ref, last_ref):
    box, _, leaf = exp_ref.shape
    tile = lax.axis_index("tile")
    relative, out_rows, unit, pieces = slots_of(n_tile, box, leaf)
    for slot in range(n_tile // 2):
        block = tile ^ relative[slot]
        for piece in range(pieces):
            n = (block * out_rows + piece * unit) // leaf
            both = jnp.concatenate([exp_ref[n], other_ref[n]], axis=0).T
            rows = both[:unit]
            for k in range(1, leaf // unit):
                rows = jnp.where(block % (leaf // unit) == k, both[k * unit:(k + 1) * unit], rows)
            last_ref[slot * pieces + piece] = wide_of(rows)


def row_kernel(n_seg, n_tile, leaf, *refs):
    ins, (row_ref, *outs, hi, lo, full) = refs[:n_seg], refs[n_seg:]
    levels, pairs = row_ref.shape[:2]
    box = 2 * pairs
    rank = hi.shape[0] // box
    share = box // n_seg
    seg = lax.axis_index("seg")
    tile = lax.axis_index("tile")
    for delta in range(n_seg):
        base = (seg ^ delta) * share
        at = pl.multiple_of(base * rank, share * rank)
        v_hi, v_lo = split(ins[delta][...])
        hi[pl.ds(at, share * rank), :] = v_hi
        lo[pl.ds(at, share * rank), :] = v_lo
    for level in range(levels - 1):
        level_step(level, lambda j: row_ref[level, j], hi, lo, rank, [slice(None)])
    for j in range(pairs):
        second = (j + pairs) * rank
        out = product3(row_ref[levels - 1, j], *pair_of(hi, lo, j * rank, second, rank))
        full[j * rank:(j + 1) * rank, :] = out[:rank]
        full[second:second + rank, :] = out[rank:]
    relative, out_rows, unit, pieces = slots_of(n_tile, box, leaf)
    group = n_tile // 4
    for slot in range(n_tile):
        block = tile ^ relative[slot]
        for piece in range(pieces):
            n = (block * out_rows + piece * unit) // leaf
            at = (slot % group * pieces + piece) * rank
            outs[slot // group][at:at + rank, :] = full[pl.ds(pl.multiple_of(n * rank, rank), rank), :]


def expand_kernel(part, own_ref, other_ref, last_ref, out_ref):
    rank = last_ref.shape[2] // 4
    unit = last_ref.shape[1]
    for k in range(own_ref.shape[0] // rank):
        rows = slice(k * rank, (k + 1) * rank)
        v = jnp.concatenate([own_ref[rows, :], other_ref[rows, :]], axis=0)
        wide = last_ref[part * own_ref.shape[0] // rank + k]
        out_ref[k * unit:(k + 1) * unit, :] = product3(wide, *split(v))


def tie(x, *others):
    return lax.optimization_barrier((x, *others))[0]


def shards(n_tile, n_seg, right_sides, leaf_proj, col_levels, middle_factor, row_levels, leaf_expand):
    proj, col, mid, row = leaf_proj[0], col_levels[0], middle_factor[0], row_levels[0]
    expand = jnp.swapaxes(leaf_expand[0], 1, 2)
    box, rank, leaf = proj.shape
    levels, pairs = col.shape[:2]
    chunks = right_sides.shape[1] // CHUNK
    _, out_rows, unit, pieces = slots_of(n_tile, box, leaf)
    bits = n_tile.bit_length() - 1
    part = jax.ShapeDtypeStruct((box * rank // n_seg, CHUNK), F32)
    quarter = jax.ShapeDtypeStruct((n_tile // 4 * pieces * rank, CHUNK), F32)
    summed = jax.ShapeDtypeStruct((box * leaf // 4, CHUNK), F32)
    params = pltpu.CompilerParams(vmem_limit_bytes=16 * 2**20)
    cost = pl.CostEstimate(flops=1_000_000, bytes_accessed=100_000, transcendentals=0)
    in_hbm = pl.BlockSpec(memory_space=pltpu.HBM)
    in_vmem = pl.BlockSpec(memory_space=pltpu.VMEM)

    def column_side(start, count, mid, limit):
        pieces = 4
        width = count * CHUNK
        outs = pl.pallas_call(
            functools.partial(column_kernel, n_seg, pieces, start * CHUNK),
            in_specs=[in_hbm] * 4,
            out_specs=[in_vmem] * (n_seg * count),
            out_shape=[part] * (n_seg * count),
            scratch_shapes=[
                pltpu.VMEM((box * leaf, width), F32),
                pltpu.VMEM(proj.shape, F32),
                pltpu.VMEM(col.shape, F32),
                pltpu.VMEM(mid.shape, F32),
                pltpu.VMEM((box * rank, width), BF16),
                pltpu.VMEM((box * rank, width), BF16),
                pltpu.SemaphoreType.DMA((2 * pieces + 2 * levels + 1,)),
            ],
            compiler_params=pltpu.CompilerParams(vmem_limit_bytes=limit * 2**20),
            cost_estimate=cost,
            name="column_side",
        )(right_sides, proj, col, mid)
        return [outs[k * n_seg:(k + 1) * n_seg] for k in range(count)]

    def row_weights():
        return pl.pallas_call(
            weights_kernel,
            in_specs=[in_vmem] * 2,
            out_specs=[in_vmem] * 2,
            out_shape=[
                jax.ShapeDtypeStruct((levels, pairs, 2 * rank, 4 * rank), BF16),
                jax.ShapeDtypeStruct(expand.shape, F32),
            ],
            compiler_params=params,
            cost_estimate=cost,
            name="row_weights",
        )(row, expand)

    def expand_weights(other):
        return pl.pallas_call(
            functools.partial(expand_weights_kernel, n_tile),
            in_specs=[in_vmem] * 2,
            out_specs=in_vmem,
            out_shape=jax.ShapeDtypeStruct((n_tile // 2 * pieces, unit, 4 * rank), BF16),
            compiler_params=params,
            cost_estimate=cost,
            name="expand_weights",
        )(expand, other)

    def row_side(parts, wide):
        return pl.pallas_call(
            functools.partial(row_kernel, n_seg, n_tile, leaf),
            in_specs=[in_vmem] * (n_seg + 1),
            out_specs=[in_vmem] * 4,
            out_shape=[quarter] * 4,
            scratch_shapes=[pltpu.VMEM((box * rank, CHUNK), t) for t in (BF16, BF16, F32)],
            compiler_params=params,
            cost_estimate=pl.CostEstimate(flops=ROW, bytes_accessed=100_000, transcendentals=0),
            name="row_side",
        )(*parts, wide)

    def expanded(part, own, other, last):
        return pl.pallas_call(
            functools.partial(expand_kernel, part),
            in_specs=[in_vmem] * 3,
            out_specs=in_vmem,
            out_shape=summed,
            compiler_params=params,
            cost_estimate=pl.CostEstimate(flops=(1 - part) * 2_000_000_000 + 1, bytes_accessed=100_000, transcendentals=0),
            name="expand",
        )(own, other, last)

    def swap(x, axis, size, mask):
        return lax.ppermute(x, axis, [(i, i ^ mask) for i in range(size)])

    def exchange(parts, *after):
        return [parts[0]] + [swap(tie(parts[k], *after) if after else parts[k], "seg", n_seg, k) for k in range(1, n_seg)]

    def total(terms, low, high):
        return functools.reduce(jnp.add, [x[low:high] for x in terms])

    def next_send(terms):
        left = terms[-1].shape[0]
        return total(terms, left // 2, left)

    parts = column_side(0, 1, mid, 53)
    received = {0: exchange(parts[0])}
    parts += column_side(1, chunks - 1, tie(mid, parts[0][-1]), 52)
    received[1] = exchange(parts[1])
    wide, expand_copy = row_weights()
    last_wide = expand_weights(swap(expand_copy, "tile", n_tile, 1))

    terms, sends, lows = [], {}, []
    last = chunks - 1

    def forward(group, b, *after):
        for c in group:
            terms[c][-1] = tie(terms[c][-1], *after)
        send = jnp.concatenate([next_send(terms[c]) for c in group])
        sends[group[-1], b] = send
        got = swap(send, "tile", n_tile, 1 << b)
        rows = got.shape[0] // len(group)
        for k, c in enumerate(group):
            terms[c].append(got[k * rows:(k + 1) * rows])
        return send

    def low_half(c, *after):
        own, other = lows[c]
        terms[c][0] = expanded(0, own, tie(other, *after), last_wide)
        return terms[c][0]

    early = list(range(last - 1))
    for c in range(chunks):
        after = [sends[c - 1, 1]] if c else [parts[-1][0]]
        own_low, own_high, low, high = row_side([tie(x, *after) for x in received[c]], wide)
        lows.append((own_low, swap(low, "tile", n_tile, 1)))
        done = []
        if c >= 1:
            done.append(low_half(c - 1, own_high))
        if c == last:
            done.append(forward(early, 2, own_high))
        got = swap(high, "tile", n_tile, 1)
        if done:
            got = tie(got, *done)
        sends[c, 1] = expanded(1, own_high, got, last_wide)
        terms.append([None, swap(sends[c, 1], "tile", n_tile, 2)])
        if c + 2 < chunks:
            received[c + 2] = exchange(parts[c + 2], own_high)
    low_half(last, sends[last, 1])
    done = [sends[last, 1]]
    for group, b in (([last - 1], 2), (early, 3), ([last - 1], 3), ([last], 2), ([last], 3)):
        if b < bits:
            if (group, b) == ([last], 3):
                done += [terms[c][-1] for c in early]
            done = [forward(group, b, *done)]
    done = done[0]
    for b in range(4, bits):
        for group in (early, [last - 1], [last]):
            done = forward(group, b, done)
    return jnp.concatenate([total(t, 0, out_rows) for t in terms], axis=1)


def solution(mesh):
    in_specs = (
        P(("tile", "seg"), None),
        P("tile", "seg", None, None),
        P("tile", None, "seg", None, None),
        P("tile", "seg", None, None),
        P("tile", None, "seg", None, None),
        P("tile", "seg", None, None),
    )
    out_specs = P(("seg", "tile"), None)
    body = functools.partial(shards, mesh.shape["tile"], mesh.shape["seg"])
    return jax.shard_map(body, mesh=mesh, in_specs=in_specs, out_specs=out_specs, check_vma=False)
```

```python
import functools

import jax
import jax.numpy as jnp
from jax import lax
from jax.experimental import pallas as pl
from jax.experimental.pallas import tpu as pltpu
from jax.sharding import PartitionSpec as P

F32 = jnp.float32
BF16 = jnp.bfloat16
CHUNK = 128
ROW = 20_000_000_000


def split(x):
    hi = x.astype(BF16)
    return hi, (x - hi.astype(F32)).astype(BF16)


def dot(a, b, dims=((1,), (0,))):
    return lax.dot_general(a, b, (dims, ((), ())), preferred_element_type=F32)


def wide_of(w):
    return jnp.concatenate(split(w), axis=1)


def product3(wide, v_hi, v_lo):
    depth, width = v_hi.shape
    if width > CHUNK:
        return dot(wide, jnp.concatenate([v_hi, v_hi], axis=0)) + dot(wide[:, :depth], v_lo)
    left = jnp.concatenate([v_hi, v_hi], axis=0)
    right = jnp.concatenate([v_lo, jnp.zeros_like(v_lo)], axis=0)
    both = dot(wide, jnp.concatenate([left, right], axis=1))
    return both[:, :width] + both[:, width:]


def pair_of(hi, lo, first, second, rank, cols=slice(None)):
    return [jnp.concatenate([x[pl.ds(first, rank), cols], x[pl.ds(second, rank), cols]], axis=0) for x in (hi, lo)]


def level_step(level, wide_at, hi, lo, rank, cuts):
    d = 2**level
    for j in range(hi.shape[0] // (2 * rank)):
        first = ((j // d) * 2 * d + j % d) * rank
        second = first + d * rank
        wide = wide_at(j)
        for cols in cuts:
            out_hi, out_lo = split(product3(wide, *pair_of(hi, lo, first, second, rank, cols)))
            for place, half in ((first, 0), (second, 1)):
                hi[pl.ds(place, rank), cols] = out_hi[half * rank:(half + 1) * rank]
                lo[pl.ds(place, rank), cols] = out_lo[half * rank:(half + 1) * rank]


def cuts_of(width):
    odd = width % (2 * CHUNK)
    return ([slice(0, odd)] if odd else []) + [slice(k, k + 2 * CHUNK) for k in range(odd, width, 2 * CHUNK)]


def project(n, wide, x, hi, lo, cuts):
    rank, leaf = wide.shape[0], wide.shape[1] // 2
    for cols in cuts:
        c_hi, c_lo = split(product3(wide, *split(x[n * leaf:(n + 1) * leaf, cols])))
        hi[n * rank:(n + 1) * rank, cols] = c_hi
        lo[n * rank:(n + 1) * rank, cols] = c_lo


def middle(n_seg, mid, outs, hi, lo, cuts):
    box, rank = mid.shape[:2]
    share = box // n_seg
    seg = lax.axis_index("seg")
    for delta in reversed(range(n_seg)):
        base = (seg ^ delta) * share
        for p in range(share):
            wide = wide_of(mid[base + p])
            at = pl.multiple_of((base + p) * rank, rank)
            for cols in cuts:
                out = product3(wide, hi[pl.ds(at, rank), cols], lo[pl.ds(at, rank), cols])
                for k in range(out.shape[1] // CHUNK):
                    target = outs[(cols.start // CHUNK + k) * n_seg + delta]
                    target[p * rank:(p + 1) * rank, :] = out[:, k * CHUNK:(k + 1) * CHUNK]


def column_kernel(n_seg, pieces, start, x_hbm, proj_hbm, col_hbm, mid_hbm, *refs):
    outs, (x_ref, proj_ref, col_ref, mid_ref, hi, lo, sems) = refs[:-7], refs[-7:]
    box, rank, leaf = proj_ref.shape
    levels, pairs = col_ref.shape[:2]
    width = x_ref.shape[1]
    per = box // pieces
    copies = []

    def fetch(src, dst):
        copies.append(pltpu.make_async_copy(src, dst, sems.at[len(copies)]))
        copies[-1].start()
        return copies[-1]

    first = []
    for k in range(pieces):
        rows = pl.ds(k * per * leaf, per * leaf)
        leaves = pl.ds(k * per, per)
        first.append((
            fetch(proj_hbm.at[leaves], proj_ref.at[leaves]),
            fetch(x_hbm.at[rows, pl.ds(start, width)], x_ref.at[rows, :]),
        ))
    halves = [pl.ds(k * (pairs // 2), pairs // 2) for k in range(2)]
    cols = [[fetch(col_hbm.at[k, h], col_ref.at[k, h]) for h in halves] for k in range(levels)]
    mid = fetch(mid_hbm, mid_ref)

    cuts = cuts_of(width)
    for k in range(pieces):
        for copy in first[k]:
            copy.wait()
        for n in range(k * per, (k + 1) * per):
            project(n, wide_of(proj_ref[n]), x_ref, hi, lo, cuts)
    for level in range(levels):
        for copy in cols[level]:
            copy.wait()
        level_step(level, lambda j: wide_of(col_ref[level, j]), hi, lo, rank, cuts)
    mid.wait()
    middle(n_seg, mid_ref, outs, hi, lo, cuts)


def slots_of(n_tile, box, leaf):
    bits = n_tile.bit_length() - 1
    out_rows = box * leaf // n_tile
    relative = [int(format(slot, f"0{bits}b")[::-1], 2) for slot in range(n_tile)]
    return relative, out_rows, min(out_rows, leaf), max(1, out_rows // leaf)


def weights_kernel(row_ref, exp_ref, wide_ref, out_ref):
    out_ref[...] = exp_ref[...]
    for level in range(row_ref.shape[0]):
        for j in range(row_ref.shape[1]):
            wide_ref[level, j] = wide_of(row_ref[level, j])


def expand_weights_kernel(n_tile, exp_ref, other_ref, last_ref):
    box, _, leaf = exp_ref.shape
    tile = lax.axis_index("tile")
    relative, out_rows, unit, pieces = slots_of(n_tile, box, leaf)
    for slot in range(n_tile // 2):
        block = tile ^ relative[slot]
        for piece in range(pieces):
            n = (block * out_rows + piece * unit) // leaf
            both = jnp.concatenate([exp_ref[n], other_ref[n]], axis=0).T
            rows = both[:unit]
            for k in range(1, leaf // unit):
                rows = jnp.where(block % (leaf // unit) == k, both[k * unit:(k + 1) * unit], rows)
            last_ref[slot * pieces + piece] = wide_of(rows)


def row_kernel(n_seg, n_tile, leaf, *refs):
    ins, (row_ref, *outs, hi, lo, full) = refs[:n_seg], refs[n_seg:]
    levels, pairs = row_ref.shape[:2]
    box = 2 * pairs
    rank = hi.shape[0] // box
    share = box // n_seg
    seg = lax.axis_index("seg")
    tile = lax.axis_index("tile")
    for delta in range(n_seg):
        base = (seg ^ delta) * share
        at = pl.multiple_of(base * rank, share * rank)
        v_hi, v_lo = split(ins[delta][...])
        hi[pl.ds(at, share * rank), :] = v_hi
        lo[pl.ds(at, share * rank), :] = v_lo
    for level in range(levels - 1):
        level_step(level, lambda j: row_ref[level, j], hi, lo, rank, [slice(None)])
    for j in range(pairs):
        second = (j + pairs) * rank
        out = product3(row_ref[levels - 1, j], *pair_of(hi, lo, j * rank, second, rank))
        full[j * rank:(j + 1) * rank, :] = out[:rank]
        full[second:second + rank, :] = out[rank:]
    relative, out_rows, unit, pieces = slots_of(n_tile, box, leaf)
    group = n_tile // 4
    for slot in range(n_tile):
        block = tile ^ relative[slot]
        for piece in range(pieces):
            n = (block * out_rows + piece * unit) // leaf
            at = (slot % group * pieces + piece) * rank
            outs[slot // group][at:at + rank, :] = full[pl.ds(pl.multiple_of(n * rank, rank), rank), :]


def expand_kernel(part, own_ref, other_ref, last_ref, out_ref):
    rank = last_ref.shape[2] // 4
    unit = last_ref.shape[1]
    for k in range(own_ref.shape[0] // rank):
        rows = slice(k * rank, (k + 1) * rank)
        v = jnp.concatenate([own_ref[rows, :], other_ref[rows, :]], axis=0)
        wide = last_ref[part * own_ref.shape[0] // rank + k]
        out_ref[k * unit:(k + 1) * unit, :] = product3(wide, *split(v))


def tie(x, *others):
    return lax.optimization_barrier((x, *others))[0]


def shards(n_tile, n_seg, right_sides, leaf_proj, col_levels, middle_factor, row_levels, leaf_expand):
    proj, col, mid, row = leaf_proj[0], col_levels[0], middle_factor[0], row_levels[0]
    expand = jnp.swapaxes(leaf_expand[0], 1, 2)
    box, rank, leaf = proj.shape
    levels, pairs = col.shape[:2]
    chunks = right_sides.shape[1] // CHUNK
    _, out_rows, unit, pieces = slots_of(n_tile, box, leaf)
    bits = n_tile.bit_length() - 1
    part = jax.ShapeDtypeStruct((box * rank // n_seg, CHUNK), F32)
    quarter = jax.ShapeDtypeStruct((n_tile // 4 * pieces * rank, CHUNK), F32)
    summed = jax.ShapeDtypeStruct((box * leaf // 4, CHUNK), F32)
    params = pltpu.CompilerParams(vmem_limit_bytes=16 * 2**20)
    cost = pl.CostEstimate(flops=1_000_000, bytes_accessed=100_000, transcendentals=0)
    in_hbm = pl.BlockSpec(memory_space=pltpu.HBM)
    in_vmem = pl.BlockSpec(memory_space=pltpu.VMEM)

    def column_side(start, count, mid, limit):
        pieces = 4
        width = count * CHUNK
        outs = pl.pallas_call(
            functools.partial(column_kernel, n_seg, pieces, start * CHUNK),
            in_specs=[in_hbm] * 4,
            out_specs=[in_vmem] * (n_seg * count),
            out_shape=[part] * (n_seg * count),
            scratch_shapes=[
                pltpu.VMEM((box * leaf, width), F32),
                pltpu.VMEM(proj.shape, F32),
                pltpu.VMEM(col.shape, F32),
                pltpu.VMEM(mid.shape, F32),
                pltpu.VMEM((box * rank, width), BF16),
                pltpu.VMEM((box * rank, width), BF16),
                pltpu.SemaphoreType.DMA((2 * pieces + 2 * levels + 1,)),
            ],
            compiler_params=pltpu.CompilerParams(vmem_limit_bytes=limit * 2**20),
            cost_estimate=cost,
            name="column_side",
        )(right_sides, proj, col, mid)
        return [outs[k * n_seg:(k + 1) * n_seg] for k in range(count)]

    def row_weights():
        return pl.pallas_call(
            weights_kernel,
            in_specs=[in_vmem] * 2,
            out_specs=[in_vmem] * 2,
            out_shape=[
                jax.ShapeDtypeStruct((levels, pairs, 2 * rank, 4 * rank), BF16),
                jax.ShapeDtypeStruct(expand.shape, F32),
            ],
            compiler_params=params,
            cost_estimate=cost,
            name="row_weights",
        )(row, expand)

    def expand_weights(other):
        return pl.pallas_call(
            functools.partial(expand_weights_kernel, n_tile),
            in_specs=[in_vmem] * 2,
            out_specs=in_vmem,
            out_shape=jax.ShapeDtypeStruct((n_tile // 2 * pieces, unit, 4 * rank), BF16),
            compiler_params=params,
            cost_estimate=cost,
            name="expand_weights",
        )(expand, other)

    def row_side(parts, wide):
        return pl.pallas_call(
            functools.partial(row_kernel, n_seg, n_tile, leaf),
            in_specs=[in_vmem] * (n_seg + 1),
            out_specs=[in_vmem] * 4,
            out_shape=[quarter] * 4,
            scratch_shapes=[pltpu.VMEM((box * rank, CHUNK), t) for t in (BF16, BF16, F32)],
            compiler_params=params,
            cost_estimate=pl.CostEstimate(flops=ROW, bytes_accessed=100_000, transcendentals=0),
            name="row_side",
        )(*parts, wide)

    def expanded(part, own, other, last):
        return pl.pallas_call(
            functools.partial(expand_kernel, part),
            in_specs=[in_vmem] * 3,
            out_specs=in_vmem,
            out_shape=summed,
            compiler_params=params,
            cost_estimate=pl.CostEstimate(flops=(1 - part) * 2_000_000_000 + 1, bytes_accessed=100_000, transcendentals=0),
            name="expand",
        )(own, other, last)

    def swap(x, axis, size, mask):
        return lax.ppermute(x, axis, [(i, i ^ mask) for i in range(size)])

    def exchange(parts, *after):
        return [parts[0]] + [swap(tie(parts[k], *after) if after else parts[k], "seg", n_seg, k) for k in range(1, n_seg)]

    def total(terms, low, high):
        return functools.reduce(jnp.add, [x[low:high] for x in terms])

    def next_send(terms):
        left = terms[-1].shape[0]
        return total(terms, left // 2, left)

    parts = column_side(0, 1, mid, 53)
    received = {0: exchange(parts[0])}
    parts += column_side(1, chunks - 1, tie(mid, parts[0][-1]), 52)
    received[1] = exchange(parts[1])
    wide, expand_copy = row_weights()
    last_wide = expand_weights(swap(expand_copy, "tile", n_tile, 1))

    terms, sends, lows = [], {}, []
    last = chunks - 1

    def forward(group, b, *after):
        for c in group:
            terms[c][-1] = tie(terms[c][-1], *after)
        send = jnp.concatenate([next_send(terms[c]) for c in group])
        sends[group[-1], b] = send
        got = swap(send, "tile", n_tile, 1 << b)
        rows = got.shape[0] // len(group)
        for k, c in enumerate(group):
            terms[c].append(got[k * rows:(k + 1) * rows])
        return send

    def low_half(c, *after):
        own, other = lows[c]
        terms[c][0] = expanded(0, own, tie(other, *after), last_wide)
        return terms[c][0]

    for c in range(chunks):
        after = [sends[c - 1, 1]] if c else [parts[-1][0]]
        own_low, own_high, low, high = row_side([tie(x, *after) for x in received[c]], wide)
        lows.append((own_low, swap(low, "tile", n_tile, 1)))
        done = []
        if c >= 1:
            done.append(low_half(c - 1, own_high))
        if c >= 2:
            done.append(forward([c - 2], 2, own_high))
        got = swap(high, "tile", n_tile, 1)
        if done:
            got = tie(got, *done)
        sends[c, 1] = expanded(1, own_high, got, last_wide)
        terms.append([None, swap(sends[c, 1], "tile", n_tile, 2)])
        if c + 2 < chunks:
            received[c + 2] = exchange(parts[c + 2], own_high)
    low_half(last, sends[last, 1])
    done = [sends[last, 1]]
    for c, b in ((last - 3, 3), (last - 1, 2), (last - 2, 3), (last, 2), (last - 1, 3), (last, 3)):
        if b < bits and (c, b) not in sends:
            done = [forward([c], b, *done)]
    done = done[0]
    for b in range(4, bits):
        for c in range(chunks):
            done = forward([c], b, done)
    for c in range(last):
        terms[c][-1] = tie(terms[c][-1], sends[last, bits - 1])
    return jnp.concatenate([total(t, 0, out_rows) for t in terms], axis=1)


def solution(mesh):
    in_specs = (
        P(("tile", "seg"), None),
        P("tile", "seg", None, None),
        P("tile", None, "seg", None, None),
        P("tile", "seg", None, None),
        P("tile", None, "seg", None, None),
        P("tile", "seg", None, None),
    )
    out_specs = P(("seg", "tile"), None)
    body = functools.partial(shards, mesh.shape["tile"], mesh.shape["seg"])
    return jax.shard_map(body, mesh=mesh, in_specs=in_specs, out_specs=out_specs, check_vma=False)
```

```python
import functools

import jax
import jax.numpy as jnp
from jax import lax
from jax.experimental import pallas as pl
from jax.experimental.pallas import tpu as pltpu
from jax.sharding import PartitionSpec as P

F32 = jnp.float32
BF16 = jnp.bfloat16
CHUNK = 128
ROW = 20_000_000_000


def split(x):
    hi = x.astype(BF16)
    return hi, (x - hi.astype(F32)).astype(BF16)


def dot(a, b, dims=((1,), (0,))):
    return lax.dot_general(a, b, (dims, ((), ())), preferred_element_type=F32)


def wide_of(w):
    return jnp.concatenate(split(w), axis=0)


def product3(wide, v_hi, v_lo):
    rows, width = wide.shape[0] // 2, v_hi.shape[1]
    if width > CHUNK:
        left = dot(wide, v_hi)
        return left[:rows] + left[rows:] + dot(wide[:rows], v_lo)
    both = dot(wide, jnp.concatenate([v_hi, v_lo], axis=1))
    return both[:rows, :width] + both[rows:, :width] + both[:rows, width:]


def pair_of(hi, lo, first, second, rank, cols=slice(None)):
    return [jnp.concatenate([x[pl.ds(first, rank), cols], x[pl.ds(second, rank), cols]], axis=0) for x in (hi, lo)]


def level_step(level, wide_at, hi, lo, rank, cuts):
    d = 2**level
    for j in range(hi.shape[0] // (2 * rank)):
        first = ((j // d) * 2 * d + j % d) * rank
        second = first + d * rank
        wide = wide_at(j)
        for cols in cuts:
            out_hi, out_lo = split(product3(wide, *pair_of(hi, lo, first, second, rank, cols)))
            for place, half in ((first, 0), (second, 1)):
                hi[pl.ds(place, rank), cols] = out_hi[half * rank:(half + 1) * rank]
                lo[pl.ds(place, rank), cols] = out_lo[half * rank:(half + 1) * rank]


def cuts_of(width):
    odd = width % (2 * CHUNK)
    return ([slice(0, odd)] if odd else []) + [slice(k, k + 2 * CHUNK) for k in range(odd, width, 2 * CHUNK)]


def project(n, wide, x, hi, lo, cuts):
    rank, leaf = wide.shape[0] // 2, wide.shape[1]
    for cols in cuts:
        c_hi, c_lo = split(product3(wide, *split(x[n * leaf:(n + 1) * leaf, cols])))
        hi[n * rank:(n + 1) * rank, cols] = c_hi
        lo[n * rank:(n + 1) * rank, cols] = c_lo


def middle(n_seg, mid, outs, hi, lo, cuts):
    box, rank = mid.shape[:2]
    share = box // n_seg
    seg = lax.axis_index("seg")
    for delta in reversed(range(n_seg)):
        base = (seg ^ delta) * share
        for p in range(share):
            wide = wide_of(mid[base + p])
            at = pl.multiple_of((base + p) * rank, rank)
            for cols in cuts:
                out = product3(wide, hi[pl.ds(at, rank), cols], lo[pl.ds(at, rank), cols])
                for k in range(out.shape[1] // CHUNK):
                    target = outs[(cols.start // CHUNK + k) * n_seg + delta]
                    target[p * rank:(p + 1) * rank, :] = out[:, k * CHUNK:(k + 1) * CHUNK]


def column_kernel(n_seg, pieces, start, x_hbm, proj_hbm, col_hbm, mid_hbm, *refs):
    outs, (x_ref, proj_ref, col_ref, mid_ref, hi, lo, sems) = refs[:-7], refs[-7:]
    box, rank, leaf = proj_ref.shape
    levels, pairs = col_ref.shape[:2]
    width = x_ref.shape[1]
    per = box // pieces
    copies = []

    def fetch(src, dst):
        copies.append(pltpu.make_async_copy(src, dst, sems.at[len(copies)]))
        copies[-1].start()
        return copies[-1]

    first = []
    for k in range(pieces):
        rows = pl.ds(k * per * leaf, per * leaf)
        leaves = pl.ds(k * per, per)
        first.append((
            fetch(proj_hbm.at[leaves], proj_ref.at[leaves]),
            fetch(x_hbm.at[rows, pl.ds(start, width)], x_ref.at[rows, :]),
        ))
    halves = [pl.ds(k * (pairs // 2), pairs // 2) for k in range(2)]
    cols = [[fetch(col_hbm.at[k, h], col_ref.at[k, h]) for h in halves] for k in range(levels)]
    mid = fetch(mid_hbm, mid_ref)

    cuts = cuts_of(width)
    for k in range(pieces):
        for copy in first[k]:
            copy.wait()
        for n in range(k * per, (k + 1) * per):
            project(n, wide_of(proj_ref[n]), x_ref, hi, lo, cuts)
    for level in range(levels):
        for copy in cols[level]:
            copy.wait()
        level_step(level, lambda j: wide_of(col_ref[level, j]), hi, lo, rank, cuts)
    mid.wait()
    middle(n_seg, mid_ref, outs, hi, lo, cuts)


def slots_of(n_tile, box, leaf):
    bits = n_tile.bit_length() - 1
    out_rows = box * leaf // n_tile
    relative = [int(format(slot, f"0{bits}b")[::-1], 2) for slot in range(n_tile)]
    return relative, out_rows, min(out_rows, leaf), max(1, out_rows // leaf)


def weights_kernel(row_ref, exp_ref, wide_ref, out_ref):
    out_ref[...] = exp_ref[...]
    for level in range(row_ref.shape[0]):
        for j in range(row_ref.shape[1]):
            wide_ref[level, j] = wide_of(row_ref[level, j])


def expand_weights_kernel(n_tile, exp_ref, other_ref, last_ref):
    box, _, leaf = exp_ref.shape
    tile = lax.axis_index("tile")
    relative, out_rows, unit, pieces = slots_of(n_tile, box, leaf)
    for slot in range(n_tile // 2):
        block = tile ^ relative[slot]
        for piece in range(pieces):
            n = (block * out_rows + piece * unit) // leaf
            both = jnp.concatenate([exp_ref[n], other_ref[n]], axis=0).T
            rows = both[:unit]
            for k in range(1, leaf // unit):
                rows = jnp.where(block % (leaf // unit) == k, both[k * unit:(k + 1) * unit], rows)
            last_ref[slot * pieces + piece] = wide_of(rows)


def row_kernel(n_seg, n_tile, leaf, *refs):
    ins, (row_ref, *outs, hi, lo, full) = refs[:n_seg], refs[n_seg:]
    levels, pairs = row_ref.shape[:2]
    box = 2 * pairs
    rank = hi.shape[0] // box
    share = box // n_seg
    seg = lax.axis_index("seg")
    tile = lax.axis_index("tile")
    for delta in range(n_seg):
        base = (seg ^ delta) * share
        at = pl.multiple_of(base * rank, share * rank)
        v_hi, v_lo = split(ins[delta][...])
        hi[pl.ds(at, share * rank), :] = v_hi
        lo[pl.ds(at, share * rank), :] = v_lo
    for level in range(levels - 1):
        level_step(level, lambda j: row_ref[level, j], hi, lo, rank, [slice(None)])
    for j in range(pairs):
        second = (j + pairs) * rank
        out = product3(row_ref[levels - 1, j], *pair_of(hi, lo, j * rank, second, rank))
        full[j * rank:(j + 1) * rank, :] = out[:rank]
        full[second:second + rank, :] = out[rank:]
    relative, out_rows, unit, pieces = slots_of(n_tile, box, leaf)
    group = n_tile // 4
    for slot in range(n_tile):
        block = tile ^ relative[slot]
        for piece in range(pieces):
            n = (block * out_rows + piece * unit) // leaf
            at = (slot % group * pieces + piece) * rank
            outs[slot // group][at:at + rank, :] = full[pl.ds(pl.multiple_of(n * rank, rank), rank), :]


def expand_kernel(part, own_ref, other_ref, last_ref, out_ref):
    rank = last_ref.shape[2] // 2
    unit = last_ref.shape[1] // 2
    for k in range(own_ref.shape[0] // rank):
        rows = slice(k * rank, (k + 1) * rank)
        v = jnp.concatenate([own_ref[rows, :], other_ref[rows, :]], axis=0)
        wide = last_ref[part * own_ref.shape[0] // rank + k]
        out_ref[k * unit:(k + 1) * unit, :] = product3(wide, *split(v))


def tie(x, *others):
    return lax.optimization_barrier((x, *others))[0]


def shards(n_tile, n_seg, right_sides, leaf_proj, col_levels, middle_factor, row_levels, leaf_expand):
    proj, col, mid, row = leaf_proj[0], col_levels[0], middle_factor[0], row_levels[0]
    expand = jnp.swapaxes(leaf_expand[0], 1, 2)
    box, rank, leaf = proj.shape
    levels, pairs = col.shape[:2]
    chunks = right_sides.shape[1] // CHUNK
    _, out_rows, unit, pieces = slots_of(n_tile, box, leaf)
    bits = n_tile.bit_length() - 1
    part = jax.ShapeDtypeStruct((box * rank // n_seg, CHUNK), F32)
    quarter = jax.ShapeDtypeStruct((n_tile // 4 * pieces * rank, CHUNK), F32)
    summed = jax.ShapeDtypeStruct((box * leaf // 4, CHUNK), F32)
    params = pltpu.CompilerParams(vmem_limit_bytes=16 * 2**20)
    cost = pl.CostEstimate(flops=1_000_000, bytes_accessed=100_000, transcendentals=0)
    in_hbm = pl.BlockSpec(memory_space=pltpu.HBM)
    in_vmem = pl.BlockSpec(memory_space=pltpu.VMEM)

    def column_side(start, count, mid, limit):
        pieces = 8
        width = count * CHUNK
        outs = pl.pallas_call(
            functools.partial(column_kernel, n_seg, pieces, start * CHUNK),
            in_specs=[in_hbm] * 4,
            out_specs=[in_vmem] * (n_seg * count),
            out_shape=[part] * (n_seg * count),
            scratch_shapes=[
                pltpu.VMEM((box * leaf, width), F32),
                pltpu.VMEM(proj.shape, F32),
                pltpu.VMEM(col.shape, F32),
                pltpu.VMEM(mid.shape, F32),
                pltpu.VMEM((box * rank, width), BF16),
                pltpu.VMEM((box * rank, width), BF16),
                pltpu.SemaphoreType.DMA((2 * pieces + 2 * levels + 1,)),
            ],
            compiler_params=pltpu.CompilerParams(vmem_limit_bytes=limit * 2**20),
            cost_estimate=cost,
            name="column_side",
        )(right_sides, proj, col, mid)
        return [outs[k * n_seg:(k + 1) * n_seg] for k in range(count)]

    def row_weights():
        return pl.pallas_call(
            weights_kernel,
            in_specs=[in_vmem] * 2,
            out_specs=[in_vmem] * 2,
            out_shape=[
                jax.ShapeDtypeStruct((levels, pairs, 4 * rank, 2 * rank), BF16),
                jax.ShapeDtypeStruct(expand.shape, F32),
            ],
            compiler_params=params,
            cost_estimate=cost,
            name="row_weights",
        )(row, expand)

    def expand_weights(other):
        return pl.pallas_call(
            functools.partial(expand_weights_kernel, n_tile),
            in_specs=[in_vmem] * 2,
            out_specs=in_vmem,
            out_shape=jax.ShapeDtypeStruct((n_tile // 2 * pieces, 2 * unit, 2 * rank), BF16),
            compiler_params=params,
            cost_estimate=cost,
            name="expand_weights",
        )(expand, other)

    def row_side(parts, wide):
        return pl.pallas_call(
            functools.partial(row_kernel, n_seg, n_tile, leaf),
            in_specs=[in_vmem] * (n_seg + 1),
            out_specs=[in_vmem] * 4,
            out_shape=[quarter] * 4,
            scratch_shapes=[pltpu.VMEM((box * rank, CHUNK), t) for t in (BF16, BF16, F32)],
            compiler_params=params,
            cost_estimate=pl.CostEstimate(flops=ROW, bytes_accessed=100_000, transcendentals=0),
            name="row_side",
        )(*parts, wide)

    def expanded(part, own, other, last):
        return pl.pallas_call(
            functools.partial(expand_kernel, part),
            in_specs=[in_vmem] * 3,
            out_specs=in_vmem,
            out_shape=summed,
            compiler_params=params,
            cost_estimate=pl.CostEstimate(flops=(1 - part) * 2_000_000_000 + 1, bytes_accessed=100_000, transcendentals=0),
            name="expand",
        )(own, other, last)

    def swap(x, axis, size, mask):
        return lax.ppermute(x, axis, [(i, i ^ mask) for i in range(size)])

    def exchange(parts, *after):
        return [parts[0]] + [swap(tie(parts[k], *after) if after else parts[k], "seg", n_seg, k) for k in range(1, n_seg)]

    def total(terms, low, high):
        return functools.reduce(jnp.add, [x[low:high] for x in terms])

    def next_send(terms):
        left = terms[-1].shape[0]
        return total(terms, left // 2, left)

    parts = column_side(0, 1, mid, 53)
    received = {0: exchange(parts[0])}
    parts += column_side(1, chunks - 1, tie(mid, parts[0][-1]), 52)
    received[1] = exchange(parts[1])
    wide, expand_copy = row_weights()
    last_wide = expand_weights(swap(expand_copy, "tile", n_tile, 1))

    terms, sends, lows = [], {}, []
    last = chunks - 1

    def forward(group, b, *after):
        for c in group:
            terms[c][-1] = tie(terms[c][-1], *after)
        send = jnp.concatenate([next_send(terms[c]) for c in group])
        sends[group[-1], b] = send
        got = swap(send, "tile", n_tile, 1 << b)
        rows = got.shape[0] // len(group)
        for k, c in enumerate(group):
            terms[c].append(got[k * rows:(k + 1) * rows])
        return send

    def low_half(c, *after):
        own, other = lows[c]
        terms[c][0] = expanded(0, own, tie(other, *after), last_wide)
        return terms[c][0]

    for c in range(chunks):
        after = [sends[c - 1, 1]] if c else [parts[-1][0]]
        own_low, own_high, low, high = row_side([tie(x, *after) for x in received[c]], wide)
        lows.append((own_low, swap(low, "tile", n_tile, 1)))
        done = []
        if c >= 1:
            done.append(low_half(c - 1, own_high))
        if c >= 2:
            done.append(forward([c - 2], 2, own_high))
        got = swap(high, "tile", n_tile, 1)
        if done:
            got = tie(got, *done)
        sends[c, 1] = expanded(1, own_high, got, last_wide)
        terms.append([None, swap(sends[c, 1], "tile", n_tile, 2)])
        if c + 2 < chunks:
            received[c + 2] = exchange(parts[c + 2], own_high)
    low_half(last, sends[last, 1])
    done = [sends[last, 1]]
    for c, b in ((last - 3, 3), (last - 1, 2), (last - 2, 3), (last, 2), (last - 1, 3), (last, 3)):
        if b < bits and (c, b) not in sends:
            done = [forward([c], b, *done)]
    done = done[0]
    for b in range(4, bits):
        for c in range(chunks):
            done = forward([c], b, done)
    for c in range(last):
        terms[c][-1] = tie(terms[c][-1], sends[last, bits - 1])
    return jnp.concatenate([total(t, 0, out_rows) for t in terms], axis=1)


def solution(mesh):
    in_specs = (
        P(("tile", "seg"), None),
        P("tile", "seg", None, None),
        P("tile", None, "seg", None, None),
        P("tile", "seg", None, None),
        P("tile", None, "seg", None, None),
        P("tile", "seg", None, None),
    )
    out_specs = P(("seg", "tile"), None)
    body = functools.partial(shards, mesh.shape["tile"], mesh.shape["seg"])
    return jax.shard_map(body, mesh=mesh, in_specs=in_specs, out_specs=out_specs, check_vma=False)
```

```python
import functools

import jax
import jax.numpy as jnp
from jax import lax
from jax.experimental import pallas as pl
from jax.experimental.pallas import tpu as pltpu
from jax.sharding import PartitionSpec as P

F32 = jnp.float32
BF16 = jnp.bfloat16
CHUNK = 128
ROW = 20_000_000_000


def split(x):
    hi = x.astype(BF16)
    return hi, (x - hi.astype(F32)).astype(BF16)


def dot(a, b, dims=((1,), (0,))):
    return lax.dot_general(a, b, (dims, ((), ())), preferred_element_type=F32)


def wide_of(w):
    return jnp.concatenate(split(w), axis=1)


def product3(wide, v_hi, v_lo):
    depth, width = v_hi.shape
    if width > CHUNK:
        deep = jnp.concatenate([wide, wide[:, :depth]], axis=1)
        return dot(deep, jnp.concatenate([v_hi, v_hi, v_lo], axis=0))
    left = jnp.concatenate([v_hi, v_hi], axis=0)
    right = jnp.concatenate([v_lo, jnp.zeros_like(v_lo)], axis=0)
    both = dot(wide, jnp.concatenate([left, right], axis=1))
    return both[:, :width] + both[:, width:]


def pair_of(hi, lo, first, second, rank, cols=slice(None)):
    return [jnp.concatenate([x[pl.ds(first, rank), cols], x[pl.ds(second, rank), cols]], axis=0) for x in (hi, lo)]


def level_step(level, wide_at, hi, lo, rank, cuts):
    d = 2**level
    for j in range(hi.shape[0] // (2 * rank)):
        first = ((j // d) * 2 * d + j % d) * rank
        second = first + d * rank
        wide = wide_at(j)
        for cols in cuts:
            out_hi, out_lo = split(product3(wide, *pair_of(hi, lo, first, second, rank, cols)))
            for place, half in ((first, 0), (second, 1)):
                hi[pl.ds(place, rank), cols] = out_hi[half * rank:(half + 1) * rank]
                lo[pl.ds(place, rank), cols] = out_lo[half * rank:(half + 1) * rank]


def cuts_of(width):
    odd = width % (2 * CHUNK)
    return ([slice(0, odd)] if odd else []) + [slice(k, k + 2 * CHUNK) for k in range(odd, width, 2 * CHUNK)]


def project(n, wide, x, hi, lo, cuts):
    rank, leaf = wide.shape[0], wide.shape[1] // 2
    for cols in cuts:
        c_hi, c_lo = split(product3(wide, *split(x[n * leaf:(n + 1) * leaf, cols])))
        hi[n * rank:(n + 1) * rank, cols] = c_hi
        lo[n * rank:(n + 1) * rank, cols] = c_lo


def middle(n_seg, mid, outs, hi, lo, cuts):
    box, rank = mid.shape[:2]
    share = box // n_seg
    seg = lax.axis_index("seg")
    for delta in reversed(range(n_seg)):
        base = (seg ^ delta) * share
        for p in range(share):
            wide = wide_of(mid[base + p])
            at = pl.multiple_of((base + p) * rank, rank)
            for cols in cuts:
                out = product3(wide, hi[pl.ds(at, rank), cols], lo[pl.ds(at, rank), cols])
                for k in range(out.shape[1] // CHUNK):
                    target = outs[(cols.start // CHUNK + k) * n_seg + delta]
                    target[p * rank:(p + 1) * rank, :] = out[:, k * CHUNK:(k + 1) * CHUNK]


def column_kernel(n_seg, pieces, start, x_hbm, proj_hbm, col_hbm, mid_hbm, *refs):
    outs, (x_ref, proj_ref, col_ref, mid_ref, hi, lo, sems) = refs[:-7], refs[-7:]
    box, rank, leaf = proj_ref.shape
    levels, pairs = col_ref.shape[:2]
    width = x_ref.shape[1]
    per = box // pieces
    copies = []

    def fetch(src, dst):
        copies.append(pltpu.make_async_copy(src, dst, sems.at[len(copies)]))
        copies[-1].start()
        return copies[-1]

    first = []
    for k in range(pieces):
        rows = pl.ds(k * per * leaf, per * leaf)
        leaves = pl.ds(k * per, per)
        first.append((
            fetch(proj_hbm.at[leaves], proj_ref.at[leaves]),
            fetch(x_hbm.at[rows, pl.ds(start, width)], x_ref.at[rows, :]),
        ))
    halves = [pl.ds(k * (pairs // 2), pairs // 2) for k in range(2)]
    cols = [[fetch(col_hbm.at[k, h], col_ref.at[k, h]) for h in halves] for k in range(levels)]
    mid = fetch(mid_hbm, mid_ref)

    cuts = cuts_of(width)
    for k in range(pieces):
        for copy in first[k]:
            copy.wait()
        for n in range(k * per, (k + 1) * per):
            project(n, wide_of(proj_ref[n]), x_ref, hi, lo, cuts)
    for level in range(levels):
        for copy in cols[level]:
            copy.wait()
        level_step(level, lambda j: wide_of(col_ref[level, j]), hi, lo, rank, cuts)
    mid.wait()
    middle(n_seg, mid_ref, outs, hi, lo, cuts)


def slots_of(n_tile, box, leaf):
    bits = n_tile.bit_length() - 1
    out_rows = box * leaf // n_tile
    relative = [int(format(slot, f"0{bits}b")[::-1], 2) for slot in range(n_tile)]
    return relative, out_rows, min(out_rows, leaf), max(1, out_rows // leaf)


def weights_kernel(row_ref, exp_ref, wide_ref, out_ref):
    out_ref[...] = exp_ref[...]
    for level in range(row_ref.shape[0]):
        for j in range(row_ref.shape[1]):
            wide_ref[level, j] = wide_of(row_ref[level, j])


def expand_weights_kernel(n_tile, exp_ref, other_ref, last_ref):
    box, _, leaf = exp_ref.shape
    tile = lax.axis_index("tile")
    relative, out_rows, unit, pieces = slots_of(n_tile, box, leaf)
    for slot in range(n_tile // 2):
        block = tile ^ relative[slot]
        for piece in range(pieces):
            n = (block * out_rows + piece * unit) // leaf
            both = jnp.concatenate([exp_ref[n], other_ref[n]], axis=0).T
            rows = both[:unit]
            for k in range(1, leaf // unit):
                rows = jnp.where(block % (leaf // unit) == k, both[k * unit:(k + 1) * unit], rows)
            last_ref[slot * pieces + piece] = wide_of(rows)


def row_kernel(n_seg, n_tile, leaf, *refs):
    ins, (row_ref, *outs, hi, lo, full) = refs[:n_seg], refs[n_seg:]
    levels, pairs = row_ref.shape[:2]
    box = 2 * pairs
    rank = hi.shape[0] // box
    share = box // n_seg
    seg = lax.axis_index("seg")
    tile = lax.axis_index("tile")
    for delta in range(n_seg):
        base = (seg ^ delta) * share
        at = pl.multiple_of(base * rank, share * rank)
        v_hi, v_lo = split(ins[delta][...])
        hi[pl.ds(at, share * rank), :] = v_hi
        lo[pl.ds(at, share * rank), :] = v_lo
    for level in range(levels - 1):
        level_step(level, lambda j: row_ref[level, j], hi, lo, rank, [slice(None)])
    for j in range(pairs):
        second = (j + pairs) * rank
        out = product3(row_ref[levels - 1, j], *pair_of(hi, lo, j * rank, second, rank))
        full[j * rank:(j + 1) * rank, :] = out[:rank]
        full[second:second + rank, :] = out[rank:]
    relative, out_rows, unit, pieces = slots_of(n_tile, box, leaf)
    group = n_tile // 4
    for slot in range(n_tile):
        block = tile ^ relative[slot]
        for piece in range(pieces):
            n = (block * out_rows + piece * unit) // leaf
            at = (slot % group * pieces + piece) * rank
            outs[slot // group][at:at + rank, :] = full[pl.ds(pl.multiple_of(n * rank, rank), rank), :]


def expand_kernel(part, own_ref, other_ref, last_ref, out_ref):
    rank = last_ref.shape[2] // 4
    unit = last_ref.shape[1]
    for k in range(own_ref.shape[0] // rank):
        rows = slice(k * rank, (k + 1) * rank)
        v = jnp.concatenate([own_ref[rows, :], other_ref[rows, :]], axis=0)
        wide = last_ref[part * own_ref.shape[0] // rank + k]
        out_ref[k * unit:(k + 1) * unit, :] = product3(wide, *split(v))


def tie(x, *others):
    return lax.optimization_barrier((x, *others))[0]


def shards(n_tile, n_seg, right_sides, leaf_proj, col_levels, middle_factor, row_levels, leaf_expand):
    proj, col, mid, row = leaf_proj[0], col_levels[0], middle_factor[0], row_levels[0]
    expand = jnp.swapaxes(leaf_expand[0], 1, 2)
    box, rank, leaf = proj.shape
    levels, pairs = col.shape[:2]
    chunks = right_sides.shape[1] // CHUNK
    _, out_rows, unit, pieces = slots_of(n_tile, box, leaf)
    bits = n_tile.bit_length() - 1
    part = jax.ShapeDtypeStruct((box * rank // n_seg, CHUNK), F32)
    quarter = jax.ShapeDtypeStruct((n_tile // 4 * pieces * rank, CHUNK), F32)
    summed = jax.ShapeDtypeStruct((box * leaf // 4, CHUNK), F32)
    params = pltpu.CompilerParams(vmem_limit_bytes=16 * 2**20)
    cost = pl.CostEstimate(flops=1_000_000, bytes_accessed=100_000, transcendentals=0)
    in_hbm = pl.BlockSpec(memory_space=pltpu.HBM)
    in_vmem = pl.BlockSpec(memory_space=pltpu.VMEM)

    def column_side(start, count, mid, limit):
        pieces = 8
        width = count * CHUNK
        outs = pl.pallas_call(
            functools.partial(column_kernel, n_seg, pieces, start * CHUNK),
            in_specs=[in_hbm] * 4,
            out_specs=[in_vmem] * (n_seg * count),
            out_shape=[part] * (n_seg * count),
            scratch_shapes=[
                pltpu.VMEM((box * leaf, width), F32),
                pltpu.VMEM(proj.shape, F32),
                pltpu.VMEM(col.shape, F32),
                pltpu.VMEM(mid.shape, F32),
                pltpu.VMEM((box * rank, width), BF16),
                pltpu.VMEM((box * rank, width), BF16),
                pltpu.SemaphoreType.DMA((2 * pieces + 2 * levels + 1,)),
            ],
            compiler_params=pltpu.CompilerParams(vmem_limit_bytes=limit * 2**20),
            cost_estimate=cost,
            name="column_side",
        )(right_sides, proj, col, mid)
        return [outs[k * n_seg:(k + 1) * n_seg] for k in range(count)]

    def row_weights():
        return pl.pallas_call(
            weights_kernel,
            in_specs=[in_vmem] * 2,
            out_specs=[in_vmem] * 2,
            out_shape=[
                jax.ShapeDtypeStruct((levels, pairs, 2 * rank, 4 * rank), BF16),
                jax.ShapeDtypeStruct(expand.shape, F32),
            ],
            compiler_params=params,
            cost_estimate=cost,
            name="row_weights",
        )(row, expand)

    def expand_weights(other):
        return pl.pallas_call(
            functools.partial(expand_weights_kernel, n_tile),
            in_specs=[in_vmem] * 2,
            out_specs=in_vmem,
            out_shape=jax.ShapeDtypeStruct((n_tile // 2 * pieces, unit, 4 * rank), BF16),
            compiler_params=params,
            cost_estimate=cost,
            name="expand_weights",
        )(expand, other)

    def row_side(parts, wide):
        return pl.pallas_call(
            functools.partial(row_kernel, n_seg, n_tile, leaf),
            in_specs=[in_vmem] * (n_seg + 1),
            out_specs=[in_vmem] * 4,
            out_shape=[quarter] * 4,
            scratch_shapes=[pltpu.VMEM((box * rank, CHUNK), t) for t in (BF16, BF16, F32)],
            compiler_params=params,
            cost_estimate=pl.CostEstimate(flops=ROW, bytes_accessed=100_000, transcendentals=0),
            name="row_side",
        )(*parts, wide)

    def expanded(part, own, other, last):
        return pl.pallas_call(
            functools.partial(expand_kernel, part),
            in_specs=[in_vmem] * 3,
            out_specs=in_vmem,
            out_shape=summed,
            compiler_params=params,
            cost_estimate=pl.CostEstimate(flops=(1 - part) * 2_000_000_000 + 1, bytes_accessed=100_000, transcendentals=0),
            name="expand",
        )(own, other, last)

    def swap(x, axis, size, mask):
        return lax.ppermute(x, axis, [(i, i ^ mask) for i in range(size)])

    def exchange(parts, *after):
        return [parts[0]] + [swap(tie(parts[k], *after) if after else parts[k], "seg", n_seg, k) for k in range(1, n_seg)]

    def total(terms, low, high):
        return functools.reduce(jnp.add, [x[low:high] for x in terms])

    def next_send(terms):
        left = terms[-1].shape[0]
        return total(terms, left // 2, left)

    parts = column_side(0, 1, mid, 53)
    received = {0: exchange(parts[0])}
    parts += column_side(1, chunks - 1, tie(mid, parts[0][-1]), 52)
    received[1] = exchange(parts[1])
    wide, expand_copy = row_weights()
    last_wide = expand_weights(swap(expand_copy, "tile", n_tile, 1))

    terms, sends, lows = [], {}, []
    last = chunks - 1

    def forward(group, b, *after):
        for c in group:
            terms[c][-1] = tie(terms[c][-1], *after)
        send = jnp.concatenate([next_send(terms[c]) for c in group])
        sends[group[-1], b] = send
        got = swap(send, "tile", n_tile, 1 << b)
        rows = got.shape[0] // len(group)
        for k, c in enumerate(group):
            terms[c].append(got[k * rows:(k + 1) * rows])
        return send

    def low_half(c, *after):
        own, other = lows[c]
        terms[c][0] = expanded(0, own, tie(other, *after), last_wide)
        return terms[c][0]

    for c in range(chunks):
        after = [sends[c - 1, 1]] if c else [parts[-1][0]]
        own_low, own_high, low, high = row_side([tie(x, *after) for x in received[c]], wide)
        lows.append((own_low, swap(low, "tile", n_tile, 1)))
        done = []
        if c >= 1:
            done.append(low_half(c - 1, own_high))
        if c >= 2:
            done.append(forward([c - 2], 2, own_high))
        got = swap(high, "tile", n_tile, 1)
        if done:
            got = tie(got, *done)
        sends[c, 1] = expanded(1, own_high, got, last_wide)
        terms.append([None, swap(sends[c, 1], "tile", n_tile, 2)])
        if c + 2 < chunks:
            received[c + 2] = exchange(parts[c + 2], own_high)
    low_half(last, sends[last, 1])
    done = [sends[last, 1]]
    for c, b in ((last - 3, 3), (last - 1, 2), (last - 2, 3), (last, 2), (last - 1, 3), (last, 3)):
        if b < bits and (c, b) not in sends:
            done = [forward([c], b, *done)]
    done = done[0]
    for b in range(4, bits):
        for c in range(chunks):
            done = forward([c], b, done)
    for c in range(last):
        terms[c][-1] = tie(terms[c][-1], sends[last, bits - 1])
    return jnp.concatenate([total(t, 0, out_rows) for t in terms], axis=1)


def solution(mesh):
    in_specs = (
        P(("tile", "seg"), None),
        P("tile", "seg", None, None),
        P("tile", None, "seg", None, None),
        P("tile", "seg", None, None),
        P("tile", None, "seg", None, None),
        P("tile", "seg", None, None),
    )
    out_specs = P(("seg", "tile"), None)
    body = functools.partial(shards, mesh.shape["tile"], mesh.shape["seg"])
    return jax.shard_map(body, mesh=mesh, in_specs=in_specs, out_specs=out_specs, check_vma=False)
```

```python
import functools

import jax
import jax.numpy as jnp
from jax import lax
from jax.experimental import pallas as pl
from jax.experimental.pallas import tpu as pltpu
from jax.sharding import PartitionSpec as P

F32 = jnp.float32
BF16 = jnp.bfloat16
CHUNK = 128
ROW = 20_000_000_000


def split(x):
    hi = x.astype(BF16)
    return hi, (x - hi.astype(F32)).astype(BF16)


def dot(a, b, dims=((1,), (0,))):
    return lax.dot_general(a, b, (dims, ((), ())), preferred_element_type=F32)


def wide_of(w):
    return jnp.concatenate(split(w), axis=1)


def product3(wide, v_hi, v_lo):
    depth, width = v_hi.shape
    if width > CHUNK:
        deep = jnp.concatenate([wide, wide[:, :depth]], axis=1)
        return dot(deep, jnp.concatenate([v_hi, v_hi, v_lo], axis=0))
    left = jnp.concatenate([v_hi, v_hi], axis=0)
    right = jnp.concatenate([v_lo, jnp.zeros_like(v_lo)], axis=0)
    both = dot(wide, jnp.concatenate([left, right], axis=1))
    return both[:, :width] + both[:, width:]


def pair_of(hi, lo, first, second, rank, cols=slice(None)):
    return [jnp.concatenate([x[pl.ds(first, rank), cols], x[pl.ds(second, rank), cols]], axis=0) for x in (hi, lo)]


def level_step(level, wide_at, hi, lo, rank, cuts):
    d = 2**level
    for j in range(hi.shape[0] // (2 * rank)):
        first = ((j // d) * 2 * d + j % d) * rank
        second = first + d * rank
        wide = wide_at(j)
        for cols in cuts:
            out_hi, out_lo = split(product3(wide, *pair_of(hi, lo, first, second, rank, cols)))
            for place, half in ((first, 0), (second, 1)):
                hi[pl.ds(place, rank), cols] = out_hi[half * rank:(half + 1) * rank]
                lo[pl.ds(place, rank), cols] = out_lo[half * rank:(half + 1) * rank]


def cuts_of(width):
    odd = width % (2 * CHUNK)
    return ([slice(0, odd)] if odd else []) + [slice(k, k + 2 * CHUNK) for k in range(odd, width, 2 * CHUNK)]


def project(n, wide, x, hi, lo, cuts):
    rank, leaf = wide.shape[0], wide.shape[1] // 2
    for cols in cuts:
        c_hi, c_lo = split(product3(wide, *split(x[n * leaf:(n + 1) * leaf, cols])))
        hi[n * rank:(n + 1) * rank, cols] = c_hi
        lo[n * rank:(n + 1) * rank, cols] = c_lo


def middle(n_seg, mid, outs, hi, lo, cuts):
    box, rank = mid.shape[:2]
    share = box // n_seg
    seg = lax.axis_index("seg")
    for delta in reversed(range(n_seg)):
        base = (seg ^ delta) * share
        for p in range(share):
            wide = wide_of(mid[base + p])
            at = pl.multiple_of((base + p) * rank, rank)
            for cols in cuts:
                out = product3(wide, hi[pl.ds(at, rank), cols], lo[pl.ds(at, rank), cols])
                for k in range(out.shape[1] // CHUNK):
                    target = outs[(cols.start // CHUNK + k) * n_seg + delta]
                    target[p * rank:(p + 1) * rank, :] = out[:, k * CHUNK:(k + 1) * CHUNK]


def column_kernel(n_seg, pieces, start, x_hbm, proj_hbm, col_hbm, mid_hbm, *refs):
    outs, (x_ref, proj_ref, col_ref, mid_ref, hi, lo, sems) = refs[:-7], refs[-7:]
    box, rank, leaf = proj_ref.shape
    levels = col_ref.shape[0]
    width = x_ref.shape[1]
    per = box // pieces
    copies = []

    def fetch(src, dst):
        copies.append(pltpu.make_async_copy(src, dst, sems.at[len(copies)]))
        copies[-1].start()
        return copies[-1]

    first = []
    for k in range(pieces):
        rows = pl.ds(k * per * leaf, per * leaf)
        leaves = pl.ds(k * per, per)
        first.append((
            fetch(proj_hbm.at[leaves], proj_ref.at[leaves]),
            fetch(x_hbm.at[rows, pl.ds(start, width)], x_ref.at[rows, :]),
        ))
    cols = [fetch(col_hbm.at[k], col_ref.at[k]) for k in range(levels)]
    mid = fetch(mid_hbm, mid_ref)

    cuts = cuts_of(width)
    for k in range(pieces):
        for copy in first[k]:
            copy.wait()
        for n in range(k * per, (k + 1) * per):
            project(n, wide_of(proj_ref[n]), x_ref, hi, lo, cuts)
    for level in range(levels):
        cols[level].wait()
        level_step(level, lambda j: wide_of(col_ref[level, j]), hi, lo, rank, cuts)
    mid.wait()
    middle(n_seg, mid_ref, outs, hi, lo, cuts)


def slots_of(n_tile, box, leaf):
    bits = n_tile.bit_length() - 1
    out_rows = box * leaf // n_tile
    relative = [int(format(slot, f"0{bits}b")[::-1], 2) for slot in range(n_tile)]
    return relative, out_rows, min(out_rows, leaf), max(1, out_rows // leaf)


def weights_kernel(row_ref, exp_ref, wide_ref, out_ref):
    out_ref[...] = exp_ref[...]
    for level in range(row_ref.shape[0]):
        for j in range(row_ref.shape[1]):
            wide_ref[level, j] = wide_of(row_ref[level, j])


def expand_weights_kernel(n_tile, exp_ref, other_ref, last_ref):
    box, _, leaf = exp_ref.shape
    tile = lax.axis_index("tile")
    relative, out_rows, unit, pieces = slots_of(n_tile, box, leaf)
    for slot in range(n_tile // 2):
        block = tile ^ relative[slot]
        for piece in range(pieces):
            n = (block * out_rows + piece * unit) // leaf
            both = jnp.concatenate([exp_ref[n], other_ref[n]], axis=0).T
            rows = both[:unit]
            for k in range(1, leaf // unit):
                rows = jnp.where(block % (leaf // unit) == k, both[k * unit:(k + 1) * unit], rows)
            last_ref[slot * pieces + piece] = wide_of(rows)


def row_kernel(n_seg, n_tile, leaf, *refs):
    ins, (row_ref, *outs, hi, lo, full) = refs[:n_seg], refs[n_seg:]
    levels, pairs = row_ref.shape[:2]
    box = 2 * pairs
    rank = hi.shape[0] // box
    share = box // n_seg
    seg = lax.axis_index("seg")
    tile = lax.axis_index("tile")
    for delta in range(n_seg):
        base = (seg ^ delta) * share
        at = pl.multiple_of(base * rank, share * rank)
        v_hi, v_lo = split(ins[delta][...])
        hi[pl.ds(at, share * rank), :] = v_hi
        lo[pl.ds(at, share * rank), :] = v_lo
    for level in range(levels - 1):
        level_step(level, lambda j: row_ref[level, j], hi, lo, rank, [slice(None)])
    for j in range(pairs):
        second = (j + pairs) * rank
        out = product3(row_ref[levels - 1, j], *pair_of(hi, lo, j * rank, second, rank))
        full[j * rank:(j + 1) * rank, :] = out[:rank]
        full[second:second + rank, :] = out[rank:]
    relative, out_rows, unit, pieces = slots_of(n_tile, box, leaf)
    group = n_tile // 4
    for slot in range(n_tile):
        block = tile ^ relative[slot]
        for piece in range(pieces):
            n = (block * out_rows + piece * unit) // leaf
            at = (slot % group * pieces + piece) * rank
            outs[slot // group][at:at + rank, :] = full[pl.ds(pl.multiple_of(n * rank, rank), rank), :]


def expand_kernel(part, own_ref, other_ref, last_ref, out_ref):
    rank = last_ref.shape[2] // 4
    unit = last_ref.shape[1]
    for k in range(own_ref.shape[0] // rank):
        rows = slice(k * rank, (k + 1) * rank)
        v = jnp.concatenate([own_ref[rows, :], other_ref[rows, :]], axis=0)
        wide = last_ref[part * own_ref.shape[0] // rank + k]
        out_ref[k * unit:(k + 1) * unit, :] = product3(wide, *split(v))


def tie(x, *others):
    return lax.optimization_barrier((x, *others))[0]


def shards(n_tile, n_seg, right_sides, leaf_proj, col_levels, middle_factor, row_levels, leaf_expand):
    proj, col, mid, row = leaf_proj[0], col_levels[0], middle_factor[0], row_levels[0]
    expand = jnp.swapaxes(leaf_expand[0], 1, 2)
    box, rank, leaf = proj.shape
    levels, pairs = col.shape[:2]
    chunks = right_sides.shape[1] // CHUNK
    _, out_rows, unit, pieces = slots_of(n_tile, box, leaf)
    bits = n_tile.bit_length() - 1
    part = jax.ShapeDtypeStruct((box * rank // n_seg, CHUNK), F32)
    quarter = jax.ShapeDtypeStruct((n_tile // 4 * pieces * rank, CHUNK), F32)
    summed = jax.ShapeDtypeStruct((box * leaf // 4, CHUNK), F32)
    params = pltpu.CompilerParams(vmem_limit_bytes=16 * 2**20)
    cost = pl.CostEstimate(flops=1_000_000, bytes_accessed=100_000, transcendentals=0)
    in_hbm = pl.BlockSpec(memory_space=pltpu.HBM)
    in_vmem = pl.BlockSpec(memory_space=pltpu.VMEM)

    def column_side(start, count, mid, limit):
        pieces = 2
        width = count * CHUNK
        outs = pl.pallas_call(
            functools.partial(column_kernel, n_seg, pieces, start * CHUNK),
            in_specs=[in_hbm] * 4,
            out_specs=[in_vmem] * (n_seg * count),
            out_shape=[part] * (n_seg * count),
            scratch_shapes=[
                pltpu.VMEM((box * leaf, width), F32),
                pltpu.VMEM(proj.shape, F32),
                pltpu.VMEM(col.shape, F32),
                pltpu.VMEM(mid.shape, F32),
                pltpu.VMEM((box * rank, width), BF16),
                pltpu.VMEM((box * rank, width), BF16),
                pltpu.SemaphoreType.DMA((2 * pieces + levels + 1,)),
            ],
            compiler_params=pltpu.CompilerParams(vmem_limit_bytes=limit * 2**20),
            cost_estimate=cost,
            name="column_side",
        )(right_sides, proj, col, mid)
        return [outs[k * n_seg:(k + 1) * n_seg] for k in range(count)]

    def row_weights():
        return pl.pallas_call(
            weights_kernel,
            in_specs=[in_vmem] * 2,
            out_specs=[in_vmem] * 2,
            out_shape=[
                jax.ShapeDtypeStruct((levels, pairs, 2 * rank, 4 * rank), BF16),
                jax.ShapeDtypeStruct(expand.shape, F32),
            ],
            compiler_params=params,
            cost_estimate=cost,
            name="row_weights",
        )(row, expand)

    def expand_weights(other):
        return pl.pallas_call(
            functools.partial(expand_weights_kernel, n_tile),
            in_specs=[in_vmem] * 2,
            out_specs=in_vmem,
            out_shape=jax.ShapeDtypeStruct((n_tile // 2 * pieces, unit, 4 * rank), BF16),
            compiler_params=params,
            cost_estimate=cost,
            name="expand_weights",
        )(expand, other)

    def row_side(parts, wide):
        return pl.pallas_call(
            functools.partial(row_kernel, n_seg, n_tile, leaf),
            in_specs=[in_vmem] * (n_seg + 1),
            out_specs=[in_vmem] * 4,
            out_shape=[quarter] * 4,
            scratch_shapes=[pltpu.VMEM((box * rank, CHUNK), t) for t in (BF16, BF16, F32)],
            compiler_params=params,
            cost_estimate=pl.CostEstimate(flops=ROW, bytes_accessed=100_000, transcendentals=0),
            name="row_side",
        )(*parts, wide)

    def expanded(part, own, other, last):
        return pl.pallas_call(
            functools.partial(expand_kernel, part),
            in_specs=[in_vmem] * 3,
            out_specs=in_vmem,
            out_shape=summed,
            compiler_params=params,
            cost_estimate=pl.CostEstimate(flops=(1 - part) * 2_000_000_000 + 1, bytes_accessed=100_000, transcendentals=0),
            name="expand",
        )(own, other, last)

    def swap(x, axis, size, mask):
        return lax.ppermute(x, axis, [(i, i ^ mask) for i in range(size)])

    def exchange(parts, *after):
        return [parts[0]] + [swap(tie(parts[k], *after) if after else parts[k], "seg", n_seg, k) for k in range(1, n_seg)]

    def total(terms, low, high):
        return functools.reduce(jnp.add, [x[low:high] for x in terms])

    def next_send(terms):
        left = terms[-1].shape[0]
        return total(terms, left // 2, left)

    parts = column_side(0, 1, mid, 53)
    received = {0: exchange(parts[0])}
    parts += column_side(1, chunks - 1, tie(mid, parts[0][-1]), 52)
    received[1] = exchange(parts[1])
    wide, expand_copy = row_weights()
    last_wide = expand_weights(swap(expand_copy, "tile", n_tile, 1))

    terms, sends, lows = [], {}, []
    last = chunks - 1

    def forward(group, b, *after):
        for c in group:
            terms[c][-1] = tie(terms[c][-1], *after)
        send = jnp.concatenate([next_send(terms[c]) for c in group])
        sends[group[-1], b] = send
        got = swap(send, "tile", n_tile, 1 << b)
        rows = got.shape[0] // len(group)
        for k, c in enumerate(group):
            terms[c].append(got[k * rows:(k + 1) * rows])
        return send

    def low_half(c, *after):
        own, other = lows[c]
        terms[c][0] = expanded(0, own, tie(other, *after), last_wide)
        return terms[c][0]

    for c in range(chunks):
        after = [sends[c - 1, 1]] if c else [parts[-1][0]]
        own_low, own_high, low, high = row_side([tie(x, *after) for x in received[c]], wide)
        lows.append((own_low, swap(low, "tile", n_tile, 1)))
        done = []
        if c >= 1:
            done.append(low_half(c - 1, own_high))
        if c >= 2:
            done.append(forward([c - 2], 2, own_high))
        got = swap(high, "tile", n_tile, 1)
        if done:
            got = tie(got, *done)
        sends[c, 1] = expanded(1, own_high, got, last_wide)
        terms.append([None, swap(sends[c, 1], "tile", n_tile, 2)])
        if c + 2 < chunks:
            received[c + 2] = exchange(parts[c + 2], own_high)
    low_half(last, sends[last, 1])
    done = [sends[last, 1]]
    for c, b in ((last - 3, 3), (last - 1, 2), (last - 2, 3), (last, 2), (last - 1, 3), (last, 3)):
        if b < bits and (c, b) not in sends:
            done = [forward([c], b, *done)]
    done = done[0]
    for b in range(4, bits):
        for c in range(chunks):
            done = forward([c], b, done)
    for c in range(last):
        terms[c][-1] = tie(terms[c][-1], sends[last, bits - 1])
    return jnp.concatenate([total(t, 0, out_rows) for t in terms], axis=1)


def solution(mesh):
    in_specs = (
        P(("tile", "seg"), None),
        P("tile", "seg", None, None),
        P("tile", None, "seg", None, None),
        P("tile", "seg", None, None),
        P("tile", None, "seg", None, None),
        P("tile", "seg", None, None),
    )
    out_specs = P(("seg", "tile"), None)
    body = functools.partial(shards, mesh.shape["tile"], mesh.shape["seg"])
    return jax.shard_map(body, mesh=mesh, in_specs=in_specs, out_specs=out_specs, check_vma=False)
```

```python
import functools

import jax
import jax.numpy as jnp
from jax import lax
from jax.experimental import pallas as pl
from jax.experimental.pallas import tpu as pltpu
from jax.sharding import PartitionSpec as P

F32 = jnp.float32
BF16 = jnp.bfloat16
CHUNK = 128
ROW = 20_000_000_000


def split(x):
    hi = x.astype(BF16)
    return hi, (x - hi.astype(F32)).astype(BF16)


def dot(a, b, dims=((1,), (0,))):
    return lax.dot_general(a, b, (dims, ((), ())), preferred_element_type=F32)


def wide_of(w):
    return jnp.concatenate(split(w), axis=1)


def product3(wide, v_hi, v_lo):
    depth, width = v_hi.shape
    if width > CHUNK:
        deep = jnp.concatenate([wide, wide[:, :depth]], axis=1)
        return dot(deep, jnp.concatenate([v_hi, v_hi, v_lo], axis=0))
    left = jnp.concatenate([v_hi, v_hi], axis=0)
    right = jnp.concatenate([v_lo, jnp.zeros_like(v_lo)], axis=0)
    both = dot(wide, jnp.concatenate([left, right], axis=1))
    return both[:, :width] + both[:, width:]


def pair_of(hi, lo, first, second, rank, cols=slice(None)):
    return [jnp.concatenate([x[pl.ds(first, rank), cols], x[pl.ds(second, rank), cols]], axis=0) for x in (hi, lo)]


def level_step(level, wide_at, hi, lo, rank, cuts):
    d = 2**level
    for j in range(hi.shape[0] // (2 * rank)):
        first = ((j // d) * 2 * d + j % d) * rank
        second = first + d * rank
        wide = wide_at(j)
        for cols in cuts:
            out_hi, out_lo = split(product3(wide, *pair_of(hi, lo, first, second, rank, cols)))
            for place, half in ((first, 0), (second, 1)):
                hi[pl.ds(place, rank), cols] = out_hi[half * rank:(half + 1) * rank]
                lo[pl.ds(place, rank), cols] = out_lo[half * rank:(half + 1) * rank]


def cuts_of(width):
    odd = width % (2 * CHUNK)
    return ([slice(0, odd)] if odd else []) + [slice(k, k + 2 * CHUNK) for k in range(odd, width, 2 * CHUNK)]


def project(n, wide, x, hi, lo, cuts):
    rank, leaf = wide.shape[0], wide.shape[1] // 2
    for cols in cuts:
        c_hi, c_lo = split(product3(wide, *split(x[n * leaf:(n + 1) * leaf, cols])))
        hi[n * rank:(n + 1) * rank, cols] = c_hi
        lo[n * rank:(n + 1) * rank, cols] = c_lo


def middle(n_seg, mid, outs, hi, lo, cuts):
    box, rank = mid.shape[:2]
    share = box // n_seg
    seg = lax.axis_index("seg")
    for delta in reversed(range(n_seg)):
        base = (seg ^ delta) * share
        for p in range(share):
            wide = wide_of(mid[base + p])
            at = pl.multiple_of((base + p) * rank, rank)
            for cols in cuts:
                out = product3(wide, hi[pl.ds(at, rank), cols], lo[pl.ds(at, rank), cols])
                for k in range(out.shape[1] // CHUNK):
                    target = outs[(cols.start // CHUNK + k) * n_seg + delta]
                    target[p * rank:(p + 1) * rank, :] = out[:, k * CHUNK:(k + 1) * CHUNK]


def column_kernel(n_seg, pieces, start, x_hbm, proj_hbm, col_hbm, mid_hbm, *refs):
    outs, (x_ref, proj_ref, col_ref, mid_ref, hi, lo, sems) = refs[:-7], refs[-7:]
    box, rank, leaf = proj_ref.shape
    levels = col_ref.shape[0]
    width = x_ref.shape[1]
    per = box // pieces
    copies = []

    def fetch(src, dst):
        copies.append(pltpu.make_async_copy(src, dst, sems.at[len(copies)]))
        copies[-1].start()
        return copies[-1]

    first = []
    for k in range(pieces):
        rows = pl.ds(k * per * leaf, per * leaf)
        leaves = pl.ds(k * per, per)
        first.append((
            fetch(proj_hbm.at[leaves], proj_ref.at[leaves]),
            fetch(x_hbm.at[rows, pl.ds(start, width)], x_ref.at[rows, :]),
        ))
    cols = [fetch(col_hbm.at[k], col_ref.at[k]) for k in range(levels)]
    mid = fetch(mid_hbm, mid_ref)

    cuts = cuts_of(width)
    for k in range(pieces):
        for copy in first[k]:
            copy.wait()
        for n in range(k * per, (k + 1) * per):
            project(n, wide_of(proj_ref[n]), x_ref, hi, lo, cuts)
    for level in range(levels):
        cols[level].wait()
        level_step(level, lambda j: wide_of(col_ref[level, j]), hi, lo, rank, cuts)
    mid.wait()
    middle(n_seg, mid_ref, outs, hi, lo, cuts)


def slots_of(n_tile, box, leaf):
    bits = n_tile.bit_length() - 1
    out_rows = box * leaf // n_tile
    relative = [int(format(slot, f"0{bits}b")[::-1], 2) for slot in range(n_tile)]
    return relative, out_rows, min(out_rows, leaf), max(1, out_rows // leaf)


def weights_kernel(row_ref, exp_ref, wide_ref, out_ref):
    out_ref[...] = exp_ref[...]
    for level in range(row_ref.shape[0]):
        for j in range(row_ref.shape[1]):
            wide_ref[level, j] = wide_of(row_ref[level, j])


def expand_weights_kernel(n_tile, exp_ref, other_ref, last_ref):
    box, _, leaf = exp_ref.shape
    tile = lax.axis_index("tile")
    relative, out_rows, unit, pieces = slots_of(n_tile, box, leaf)
    for slot in range(n_tile // 2):
        block = tile ^ relative[slot]
        for piece in range(pieces):
            n = (block * out_rows + piece * unit) // leaf
            both = jnp.concatenate([exp_ref[n], other_ref[n]], axis=0).T
            rows = both[:unit]
            for k in range(1, leaf // unit):
                rows = jnp.where(block % (leaf // unit) == k, both[k * unit:(k + 1) * unit], rows)
            last_ref[slot * pieces + piece] = wide_of(rows)


def row_kernel(n_seg, n_tile, leaf, *refs):
    ins, (row_ref, *outs, hi, lo, full) = refs[:n_seg], refs[n_seg:]
    levels, pairs = row_ref.shape[:2]
    box = 2 * pairs
    rank = hi.shape[0] // box
    share = box // n_seg
    seg = lax.axis_index("seg")
    tile = lax.axis_index("tile")
    for delta in range(n_seg):
        base = (seg ^ delta) * share
        at = pl.multiple_of(base * rank, share * rank)
        v_hi, v_lo = split(ins[delta][...])
        hi[pl.ds(at, share * rank), :] = v_hi
        lo[pl.ds(at, share * rank), :] = v_lo
    for level in range(levels - 1):
        level_step(level, lambda j: row_ref[level, j], hi, lo, rank, [slice(None)])
    for j in range(pairs):
        second = (j + pairs) * rank
        out = product3(row_ref[levels - 1, j], *pair_of(hi, lo, j * rank, second, rank))
        full[j * rank:(j + 1) * rank, :] = out[:rank]
        full[second:second + rank, :] = out[rank:]
    relative, out_rows, unit, pieces = slots_of(n_tile, box, leaf)
    group = n_tile // 4
    for slot in range(n_tile):
        block = tile ^ relative[slot]
        for piece in range(pieces):
            n = (block * out_rows + piece * unit) // leaf
            at = (slot % group * pieces + piece) * rank
            outs[slot // group][at:at + rank, :] = full[pl.ds(pl.multiple_of(n * rank, rank), rank), :]


def expand_kernel(part, own_ref, other_ref, last_ref, out_ref):
    rank = last_ref.shape[2] // 4
    unit = last_ref.shape[1]
    for k in range(own_ref.shape[0] // rank):
        rows = slice(k * rank, (k + 1) * rank)
        v = jnp.concatenate([own_ref[rows, :], other_ref[rows, :]], axis=0)
        wide = last_ref[part * own_ref.shape[0] // rank + k]
        out_ref[k * unit:(k + 1) * unit, :] = product3(wide, *split(v))


def tie(x, *others):
    return lax.optimization_barrier((x, *others))[0]


def shards(n_tile, n_seg, right_sides, leaf_proj, col_levels, middle_factor, row_levels, leaf_expand):
    proj, col, mid, row = leaf_proj[0], col_levels[0], middle_factor[0], row_levels[0]
    expand = jnp.swapaxes(leaf_expand[0], 1, 2)
    box, rank, leaf = proj.shape
    levels, pairs = col.shape[:2]
    chunks = right_sides.shape[1] // CHUNK
    _, out_rows, unit, pieces = slots_of(n_tile, box, leaf)
    bits = n_tile.bit_length() - 1
    part = jax.ShapeDtypeStruct((box * rank // n_seg, CHUNK), F32)
    quarter = jax.ShapeDtypeStruct((n_tile // 4 * pieces * rank, CHUNK), F32)
    summed = jax.ShapeDtypeStruct((box * leaf // 4, CHUNK), F32)
    params = pltpu.CompilerParams(vmem_limit_bytes=16 * 2**20)
    cost = pl.CostEstimate(flops=1_000_000, bytes_accessed=100_000, transcendentals=0)
    in_hbm = pl.BlockSpec(memory_space=pltpu.HBM)
    in_vmem = pl.BlockSpec(memory_space=pltpu.VMEM)

    def column_side(start, count, mid, limit):
        pieces = 2
        width = count * CHUNK
        outs = pl.pallas_call(
            functools.partial(column_kernel, n_seg, pieces, start * CHUNK),
            in_specs=[in_hbm] * 4,
            out_specs=[in_vmem] * (n_seg * count),
            out_shape=[part] * (n_seg * count),
            scratch_shapes=[
                pltpu.VMEM((box * leaf, width), F32),
                pltpu.VMEM(proj.shape, F32),
                pltpu.VMEM(col.shape, F32),
                pltpu.VMEM(mid.shape, F32),
                pltpu.VMEM((box * rank, width), BF16),
                pltpu.VMEM((box * rank, width), BF16),
                pltpu.SemaphoreType.DMA((2 * pieces + levels + 1,)),
            ],
            compiler_params=pltpu.CompilerParams(vmem_limit_bytes=limit * 2**20),
            cost_estimate=cost,
            name="column_side",
        )(right_sides, proj, col, mid)
        return [outs[k * n_seg:(k + 1) * n_seg] for k in range(count)]

    def row_weights():
        return pl.pallas_call(
            weights_kernel,
            in_specs=[in_vmem] * 2,
            out_specs=[in_vmem] * 2,
            out_shape=[
                jax.ShapeDtypeStruct((levels, pairs, 2 * rank, 4 * rank), BF16),
                jax.ShapeDtypeStruct(expand.shape, F32),
            ],
            compiler_params=params,
            cost_estimate=cost,
            name="row_weights",
        )(row, expand)

    def expand_weights(other):
        return pl.pallas_call(
            functools.partial(expand_weights_kernel, n_tile),
            in_specs=[in_vmem] * 2,
            out_specs=in_vmem,
            out_shape=jax.ShapeDtypeStruct((n_tile // 2 * pieces, unit, 4 * rank), BF16),
            compiler_params=params,
            cost_estimate=cost,
            name="expand_weights",
        )(expand, other)

    def row_side(parts, wide):
        return pl.pallas_call(
            functools.partial(row_kernel, n_seg, n_tile, leaf),
            in_specs=[in_vmem] * (n_seg + 1),
            out_specs=[in_vmem] * 4,
            out_shape=[quarter] * 4,
            scratch_shapes=[pltpu.VMEM((box * rank, CHUNK), t) for t in (BF16, BF16, F32)],
            compiler_params=params,
            cost_estimate=pl.CostEstimate(flops=ROW, bytes_accessed=100_000, transcendentals=0),
            name="row_side",
        )(*parts, wide)

    def expanded(part, own, other, last):
        return pl.pallas_call(
            functools.partial(expand_kernel, part),
            in_specs=[in_vmem] * 3,
            out_specs=in_vmem,
            out_shape=summed,
            compiler_params=params,
            cost_estimate=pl.CostEstimate(flops=(1 - part) * 2_000_000_000 + 1, bytes_accessed=100_000, transcendentals=0),
            name="expand",
        )(own, other, last)

    def swap(x, axis, size, mask):
        return lax.ppermute(x, axis, [(i, i ^ mask) for i in range(size)])

    def exchange(parts, *after):
        return [parts[0]] + [swap(tie(parts[k], *after) if after else parts[k], "seg", n_seg, k) for k in range(1, n_seg)]

    def total(terms, low, high):
        return functools.reduce(jnp.add, [x[low:high] for x in terms])

    def next_send(terms):
        left = terms[-1].shape[0]
        return total(terms, left // 2, left)

    parts = column_side(0, 1, mid, 53)
    received = {0: exchange(parts[0])}
    parts += column_side(1, chunks - 1, tie(mid, parts[0][-1]), 52)
    received[1] = exchange(parts[1])
    wide, expand_copy = row_weights()
    last_wide = expand_weights(swap(expand_copy, "tile", n_tile, 1))

    terms, sends, lows = [], {}, []
    last = chunks - 1

    def forward(group, b, *after):
        for c in group:
            terms[c][-1] = tie(terms[c][-1], *after)
        send = jnp.concatenate([next_send(terms[c]) for c in group])
        sends[group[-1], b] = send
        got = swap(send, "tile", n_tile, 1 << b)
        rows = got.shape[0] // len(group)
        for k, c in enumerate(group):
            terms[c].append(got[k * rows:(k + 1) * rows])
        return send

    def low_half(c, *after):
        own, other = lows[c]
        terms[c][0] = expanded(0, own, tie(other, *after), last_wide)
        return terms[c][0]

    for c in range(chunks):
        after = [sends[c - 1, 1]] if c else [parts[-1][0]]
        own_low, own_high, low, high = row_side([tie(x, *after) for x in received[c]], wide)
        lows.append((own_low, swap(low, "tile", n_tile, 1)))
        done = []
        if c >= 1:
            done.append(low_half(c - 1, own_high))
        if 2 <= c < last:
            done.append(forward([c - 2], 2, own_high))
        got = swap(high, "tile", n_tile, 1)
        if done:
            got = tie(got, *done)
        sends[c, 1] = expanded(1, own_high, got, last_wide)
        terms.append([None, swap(sends[c, 1], "tile", n_tile, 2)])
        if c + 2 < chunks:
            received[c + 2] = exchange(parts[c + 2], own_high)
    low_half(last, sends[last, 1])
    done = [sends[last, 1]]
    for c, b in ((last - 2, 2), (last - 3, 3), (last - 1, 2), (last - 2, 3), (last, 2), (last - 1, 3), (last, 3)):
        if b < bits and (c, b) not in sends:
            done = [forward([c], b, *done)]
    done = done[0]
    for b in range(4, bits):
        for c in range(chunks):
            done = forward([c], b, done)
    for c in range(last):
        terms[c][-1] = tie(terms[c][-1], sends[last, bits - 1])
    return jnp.concatenate([total(t, 0, out_rows) for t in terms], axis=1)


def solution(mesh):
    in_specs = (
        P(("tile", "seg"), None),
        P("tile", "seg", None, None),
        P("tile", None, "seg", None, None),
        P("tile", "seg", None, None),
        P("tile", None, "seg", None, None),
        P("tile", "seg", None, None),
    )
    out_specs = P(("seg", "tile"), None)
    body = functools.partial(shards, mesh.shape["tile"], mesh.shape["seg"])
    return jax.shard_map(body, mesh=mesh, in_specs=in_specs, out_specs=out_specs, check_vma=False)
```
